128 devices in a mesh: dp: 16 (over y, z), ulysses: 8 (over x, core).
Axes of the slice: x: 4, y: 4, z: 4, core: 2. Of those that a mesh axis runs over, the one named last changes fastest.
Arguments:
- query_vectors: bfloat16 [32768, 3072], P(('dp', 'ulysses')), may hold values from -20 to 20
- key_vectors: bfloat16 [32768, 3072], P(('dp', 'ulysses')), may hold values from -20 to 20
- value_vectors: bfloat16 [32768, 3072], P(('dp', 'ulysses')), may hold values from -6 to 6
- query_tangent: bfloat16 [32768, 3072], P(('dp', 'ulysses')), may hold values from -6 to 6
- key_tangent: bfloat16 [32768, 3072], P(('dp', 'ulysses')), may hold values from -6 to 6
- value_tangent: bfloat16 [32768, 3072], P(('dp', 'ulysses')), may hold values from -6 to 6
- out_weight: bfloat16 [3072, 3072], P(('dp', 'ulysses')), may hold values from -0.3125 to 0.3125
- frame_counts: int32 [32], replicated, may hold values from 1 to 8, as said below
- token_offsets: int32 [32], replicated, may hold values from 0 to 1024
- video_group: int32 [32], replicated, may hold values from 0 to 15
Outputs:
- block_out: bfloat16 [32768, 3072], P(('dp', 'ulysses'))
- block_tangent: bfloat16 [32768, 3072], P(('dp', 'ulysses'))
The draws below stay inside these ranges and needn't reach their ends.
Inputs may be any that keep to these rules, and one draw needn't show every extreme that they name: `frame_counts`: each data group holds exactly two videos packed from its first slot: one at offset 0, the other starting where that one ends; a video has 128 tokens a frame, and one video has exactly 8 frames.
All inputs are finite; a program needn't handle non-finite values.
Results may differ from the reference program's by a relative error of at most 0.0057.
Values may be sent and summed in bfloat16 or wider, within the bound.
No kernel may reach another device: no remote copies, remote signals or barrier semaphores. Data moves between devices by JAX's collectives and lax.ppermute only.
A program may use at most 128 MiB of HBM per device.

```python
import math
import jax
import jax.numpy as jnp
from jax import lax

HEADS = 24
HEAD_DIM = 128
OUT_WIDTH = 3072
TOK_DEV = 256
FRAME_TOKENS = 128
ATTN_WIDTH = 3072
TOKENS = 32768
VIDEOS = 32
FRAMES_MOST = 8
N_DP = 16
N_ULYSSES = 8


def video_plan(key):
    count_key, place_key, long_key = jax.random.split(key, 3)
    cube_base = jax.random.randint(count_key, (VIDEOS,), 0, 16)
    counts = 1 + cube_base * cube_base * cube_base * (FRAMES_MOST - 1) // 3375
    longest = jax.random.randint(long_key, (), 0, VIDEOS)
    index_row = jnp.arange(VIDEOS)
    counts = jnp.where(index_row == longest, FRAMES_MOST, counts).astype(jnp.int32)
    placing = jax.random.permutation(place_key, VIDEOS).astype(jnp.int32)
    long_place = placing[longest]
    even_place = long_place - long_place % 2
    placing = jnp.where(index_row == longest, even_place, jnp.where(placing == even_place, long_place, placing)).astype(jnp.int32)
    inverse = jnp.argsort(placing).astype(jnp.int32)
    partner = inverse[jnp.bitwise_xor(placing, 1)]
    offsets = jnp.where(placing % 2 == 1, counts[partner] * FRAME_TOKENS, 0).astype(jnp.int32)
    groups = (placing // 2).astype(jnp.int32)
    return (counts, offsets, groups)


def draw_frame_counts(key, part):
    plan = video_plan(key)
    return plan[0]


def draw_token_offsets(key, part):
    plan = video_plan(key)
    return plan[1]


def draw_video_group(key, part):
    plan = video_plan(key)
    return plan[2]


def draw_query_vectors(key, part):
    key = jax.random.fold_in(key, 1)
    result = 1.5 * jnp.clip(jax.random.normal(key, (TOKENS, ATTN_WIDTH), jnp.float32), -4.0, 4.0)
    return result.astype(jnp.bfloat16)


def draw_key_vectors(key, part):
    key = jax.random.fold_in(key, 2)
    result = 1.5 * jnp.clip(jax.random.normal(key, (TOKENS, ATTN_WIDTH), jnp.float32), -4.0, 4.0)
    return result.astype(jnp.bfloat16)


def steps_of(stream_key, shape, shards, least, high):
    factor_of, own = 1.0, jax.random.fold_in(stream_key, 6)
    for axis_at, blocks in shards:
        draws = jnp.exp(jax.random.uniform(jax.random.fold_in(own, axis_at), (blocks,), jnp.float32, least / len(shards), high / len(shards)))
        factor_of = factor_of * jnp.repeat(draws, shape[axis_at] // blocks).reshape([-1 if axis == axis_at else 1 for axis in range(len(shape))])
    return factor_of


def centred(stream_key, extent, spread, bound, pieces=(), kind=jnp.bfloat16):
    array = jax.random.normal(stream_key, extent, jnp.float32) * spread
    if len(pieces) > 0:
        array = steps_of(stream_key, extent, pieces, -0.22, 0.18) * array
    return jnp.clip(array, min=-bound, max=bound).astype(kind)


def setup_inputs(seed: int = 0) -> dict:
    streams_of = jax.random.split(jax.random.key(seed), 11)
    query_vectors = draw_query_vectors(jax.random.fold_in(streams_of[10], 71), 0)
    key_vectors = draw_key_vectors(jax.random.fold_in(streams_of[10], 71), 0)
    value_vectors = centred(streams_of[2], (TOKENS, ATTN_WIDTH), 1.0, 6.0, ((0, 128),))
    query_tangent = centred(streams_of[3], (TOKENS, ATTN_WIDTH), 1.0, 6.0, ((0, 128),))
    key_tangent = centred(streams_of[4], (TOKENS, ATTN_WIDTH), 1.0, 6.0, ((0, 128),))
    value_tangent = centred(streams_of[5], (TOKENS, ATTN_WIDTH), 1.0, 6.0, ((0, 128),))
    out_weight = centred(streams_of[6], (ATTN_WIDTH, OUT_WIDTH), (ATTN_WIDTH // 8) ** -0.5, 0.3125, ((0, 128),))
    frame_counts = draw_frame_counts(jax.random.fold_in(streams_of[10], 71), 0)
    token_offsets = draw_token_offsets(jax.random.fold_in(streams_of[10], 71), 0)
    video_group = draw_video_group(jax.random.fold_in(streams_of[10], 71), 0)
    return dict(query_vectors=query_vectors, key_vectors=key_vectors, value_vectors=value_vectors, query_tangent=query_tangent, key_tangent=key_tangent, value_tangent=value_tangent, out_weight=out_weight, frame_counts=frame_counts, token_offsets=token_offsets, video_group=video_group)


masked_value = -1e+30

def segment_ids(frame_counts, token_offsets, video_group, group_index, seq_length):
    position = jnp.arange(seq_length, dtype=jnp.int32)[:, None]
    starts = token_offsets[None, :]
    member = (video_group[None, :] == group_index) & (position >= starts) & (position < starts + FRAME_TOKENS * frame_counts[None, :])
    video_labels = jnp.arange(1, frame_counts.shape[0] + 1, dtype=jnp.int32)[None, :]
    return lax.optimization_barrier(jnp.sum(jnp.where(member, video_labels, 0), axis=1)).astype(jnp.int32)

def block_attention(query_rows, keys_head, values_head, tquery_rows, tkeys_head, tvalues_head, row_labels, key_labels):
    scale_factor = 1.0 / math.sqrt(query_rows.shape[-1])
    scores = jnp.dot(query_rows, keys_head.T, preferred_element_type=jnp.float32) * scale_factor
    tangent_scores = (jnp.dot(tquery_rows, keys_head.T, preferred_element_type=jnp.float32) + jnp.dot(query_rows, tkeys_head.T, preferred_element_type=jnp.float32)) * scale_factor
    allowed = (row_labels[:, None] == key_labels[None, :]) & (row_labels[:, None] > 0)
    scores = jnp.where(allowed, scores, masked_value)
    row_max = lax.optimization_barrier(jnp.max(scores, axis=1, keepdims=True))
    weights = jnp.exp(scores - row_max)
    probabilities = weights / lax.optimization_barrier(jnp.sum(weights, axis=1, keepdims=True))
    probs_low = probabilities.astype(jnp.bfloat16)
    primal_out = jnp.dot(probs_low, values_head, preferred_element_type=jnp.float32)
    mean_tangent = lax.optimization_barrier(jnp.sum(probabilities * tangent_scores, axis=1, keepdims=True))
    tangent_probs = (probabilities * (tangent_scores - mean_tangent)).astype(jnp.bfloat16)
    tangent_out = jnp.dot(tangent_probs, values_head, preferred_element_type=jnp.float32) + jnp.dot(probs_low, tvalues_head, preferred_element_type=jnp.float32)
    valid_rows = (row_labels > 0)[:, None]
    return (jnp.where(valid_rows, primal_out, 0.0).astype(jnp.bfloat16), jnp.where(valid_rows, tangent_out, 0.0).astype(jnp.bfloat16))

def head_attention(queries_head, keys_head, values_head, tqueries_head, tkeys_head, tvalues_head, token_labels):
    seq_length = queries_head.shape[0]
    block_rows = min(512, seq_length)
    block_count = seq_length // block_rows
    query_blocks = queries_head.reshape(block_count, block_rows, -1)
    tquery_blocks = tqueries_head.reshape(block_count, block_rows, -1)
    label_blocks = token_labels.reshape(block_count, block_rows)

    def one_block(block_items):
        return block_attention(block_items[0], keys_head, values_head, block_items[1], tkeys_head, tvalues_head, block_items[2], token_labels)
    primal, tangent = lax.map(one_block, (query_blocks, tquery_blocks, label_blocks))
    return (primal.reshape(seq_length, -1), tangent.reshape(seq_length, -1))

def reference(query_vectors, key_vectors, value_vectors, query_tangent, key_tangent, value_tangent, out_weight, frame_counts, token_offsets, video_group):
    seq_length = N_ULYSSES * TOK_DEV
    inputs_all = (query_vectors, key_vectors, value_vectors, query_tangent, key_tangent, value_tangent)

    def per_group(group_index):
        token_labels = segment_ids(frame_counts, token_offsets, video_group, group_index, seq_length)
        first_row = (group_index * seq_length).astype(jnp.int32)
        group_rows = [lax.dynamic_slice_in_dim(tensor, first_row, seq_length, 0).reshape(seq_length, HEADS, HEAD_DIM) for tensor in inputs_all]

        def per_head(head_number):
            head_slices = [lax.dynamic_index_in_dim(tensor, head_number, 1, keepdims=False) for tensor in group_rows]
            return head_attention(*head_slices, token_labels)
        primal, tangent = lax.map(per_head, jnp.arange(HEADS, dtype=jnp.int32))
        primal = primal.transpose(1, 0, 2).reshape(seq_length, HEADS * HEAD_DIM)
        tangent = tangent.transpose(1, 0, 2).reshape(seq_length, HEADS * HEAD_DIM)
        return (primal, tangent)
    primal, tangent = lax.map(per_group, jnp.arange(N_DP, dtype=jnp.int32))
    primal = primal.reshape(N_DP * seq_length, HEADS * HEAD_DIM)
    tangent = tangent.reshape(N_DP * seq_length, HEADS * HEAD_DIM)
    block_out = jnp.dot(primal, out_weight, preferred_element_type=jnp.float32).astype(jnp.bfloat16)
    block_tangent = jnp.dot(tangent, out_weight, preferred_element_type=jnp.float32).astype(jnp.bfloat16)
    return (block_out, block_tangent)
```

```python
import functools
import math

import jax
import jax.numpy as jnp
from jax import lax
from jax.experimental import pallas as pl
from jax.experimental.pallas import tpu as pltpu
from jax.sharding import PartitionSpec as P

HEAD_DIM = 128
FRAME = 128
FRAMES_MOST = 8
LOG2E = 1.4426950408889634


def pack_kernel(q, k, v, dq, dk, dv, out):
    for i, ref in enumerate((q, k, v, dq, dk, dv)):
        out[0, i] = ref[...]


def pack_round(tensors, first, rounds, members):
    rows = tensors[0].shape[0]
    return pl.pallas_call(
        pack_kernel,
        grid=(members,),
        in_specs=[pl.BlockSpec((rows, HEAD_DIM), lambda u: (0, u * rounds + first))] * 6,
        out_specs=pl.BlockSpec((1, 6, rows, HEAD_DIM), lambda u: (u, 0, 0, 0)),
        out_shape=jax.ShapeDtypeStruct((members, 6, rows, HEAD_DIM), jnp.bfloat16),
        name="pack",
    )(*tensors)


def nt_dot(a, b):
    return lax.dot_general(a, b, (((1,), (1,)), ((), ())), preferred_element_type=jnp.float32)


def attend_kernel(info, x, out, qq, kk, vv):
    members, _, rows, _ = x.shape
    per = rows // FRAME
    first_count, second_count = info[0], info[1]
    used = first_count + second_count
    factor = LOG2E / math.sqrt(HEAD_DIM)
    scale = 1.0 / math.sqrt(HEAD_DIM)

    def gather(u, carry):
        at = pl.ds(pl.multiple_of(u * rows, rows), rows)
        qq[at, :HEAD_DIM] = x[u, 3]
        qq[at, HEAD_DIM:] = x[u, 0]
        kk[at, :HEAD_DIM] = x[u, 1]
        kk[at, HEAD_DIM:] = x[u, 4]
        vv[at, :HEAD_DIM] = x[u, 2]
        vv[at, HEAD_DIM:] = x[u, 5]
        return carry

    lax.fori_loop(0, (used + per - 1) // per, gather, 0)

    def store(frame, which, value):
        half = pl.multiple_of(lax.rem(frame, per) * FRAME, FRAME)
        out[lax.div(frame, per), which, pl.ds(half, FRAME), :] = value

    def one_video(start, count):
        keys = pl.ds(pl.multiple_of(start * FRAME, FRAME), count * FRAME)

        def one_frame(i, carry):
            frame = start + i
            at = pl.ds(pl.multiple_of(frame * FRAME, FRAME), FRAME)
            s = nt_dot(qq[at, HEAD_DIM:], kk[keys, :HEAD_DIM]) * factor
            t = nt_dot(qq[at, :], kk[keys, :]) * scale
            e = jnp.exp2(s - jnp.max(s, axis=1, keepdims=True))
            total = 1.0 / jnp.sum(e, axis=1, keepdims=True)
            mean = jnp.sum(e * t, axis=1, keepdims=True) * total
            low = e.astype(jnp.bfloat16)
            turned = (e * (t - mean)).astype(jnp.bfloat16)
            both = jnp.dot(low, vv[keys, :], preferred_element_type=jnp.float32)
            more = jnp.dot(turned, vv[keys, :HEAD_DIM], preferred_element_type=jnp.float32)
            store(frame, 0, (both[:, :HEAD_DIM] * total).astype(jnp.bfloat16))
            store(frame, 1, ((both[:, HEAD_DIM:] + more) * total).astype(jnp.bfloat16))
            return carry

        lax.fori_loop(0, count, one_frame, 0)

    def video(i, carry):
        start = jnp.where(i == 0, 0, first_count)
        count = jnp.where(i == 0, first_count, second_count)
        for n in range(1, FRAMES_MOST + 1):
            pl.when(count == n)(functools.partial(one_video, start, n))
        return carry

    lax.fori_loop(0, 2, video, 0)

    def blank(frame, carry):
        nothing = jnp.zeros((FRAME, HEAD_DIM), jnp.bfloat16)
        store(frame, 0, nothing)
        store(frame, 1, nothing)
        return carry

    lax.fori_loop(used, members * per, blank, 0)


def attend(info, x):
    members, _, rows, _ = x.shape
    tokens = members * rows
    return pl.pallas_call(
        attend_kernel,
        in_specs=[
            pl.BlockSpec(memory_space=pltpu.SMEM),
            pl.BlockSpec(memory_space=pltpu.VMEM),
        ],
        out_specs=pl.BlockSpec(memory_space=pltpu.VMEM),
        out_shape=jax.ShapeDtypeStruct((members, 2, rows, HEAD_DIM), jnp.bfloat16),
        scratch_shapes=[pltpu.VMEM((tokens, 2 * HEAD_DIM), jnp.bfloat16)] * 3,
        compiler_params=pltpu.CompilerParams(vmem_limit_bytes=40 * 2**20),
        cost_estimate=pl.CostEstimate(
            flops=7 * 10**9, bytes_accessed=4 * 2**20, transcendentals=2**21
        ),
        name="attend",
    )(info, x)


def project_kernel(rounds, *refs):
    moved, (w, out, tangent, held) = refs[:rounds], refs[rounds:]
    members, _, rows, _ = moved[0].shape

    @pl.when(pl.program_id(0) == 0)
    def _():
        for r, ref in enumerate(moved):
            for u in range(members):
                head = (u * rounds + r) * HEAD_DIM
                for which in range(2):
                    held[which * rows : (which + 1) * rows, head : head + HEAD_DIM] = ref[u, which]

    product = jnp.dot(held[...], w[...], preferred_element_type=jnp.float32)
    out[...] = product[:rows].astype(jnp.bfloat16)
    tangent[...] = product[rows:].astype(jnp.bfloat16)


def project(moved, w):
    rounds = len(moved)
    members, _, rows, _ = moved[0].shape
    depth, width = w.shape
    tile = 512
    given = pl.BlockSpec((rows, tile), lambda n: (0, n))
    return pl.pallas_call(
        functools.partial(project_kernel, rounds),
        grid=(width // tile,),
        in_specs=[pl.BlockSpec(memory_space=pltpu.VMEM)] * rounds
        + [pl.BlockSpec((depth, tile), lambda n: (0, n))],
        out_specs=[given, given],
        out_shape=[jax.ShapeDtypeStruct((rows, width), jnp.bfloat16)] * 2,
        scratch_shapes=[pltpu.VMEM((2 * rows, depth), jnp.bfloat16)],
        compiler_params=pltpu.CompilerParams(vmem_limit_bytes=40 * 2**20),
        name="project",
    )(*moved, w)


def exchange(x):
    return lax.all_to_all(x, "ulysses", split_axis=0, concat_axis=0, tiled=True)


def shards(q, k, v, dq, dk, dv, out_weight, frame_counts, token_offsets, video_group):
    members = lax.axis_size("ulysses")
    rounds = q.shape[1] // HEAD_DIM // members
    mine = video_group == lax.axis_index("dp")
    info = jnp.stack(
        [
            jnp.sum(jnp.where(mine & (token_offsets == 0), frame_counts, 0)),
            jnp.sum(jnp.where(mine & (token_offsets > 0), frame_counts, 0)),
        ]
    ).astype(jnp.int32)
    weight = lax.all_gather(out_weight, ("dp", "ulysses"), axis=0, tiled=True)
    moved = []
    for r in range(rounds):
        arrived = exchange(pack_round((q, k, v, dq, dk, dv), r, rounds, members))
        moved.append(exchange(attend(info, arrived)))
    return tuple(project(moved, weight))


def solution(mesh):
    split = P(("dp", "ulysses"), None)
    return jax.shard_map(
        shards,
        mesh=mesh,
        in_specs=(split,) * 7 + (P(),) * 3,
        out_specs=(split, split),
        check_vma=False,
    )
```

```python
import functools
import math

import jax
import jax.numpy as jnp
from jax import lax
from jax.experimental import pallas as pl
from jax.experimental.pallas import tpu as pltpu
from jax.sharding import PartitionSpec as P

HEAD_DIM = 128
FRAME = 128
FRAMES_MOST = 8
CORES = 2
LOG2E = 1.4426950408889634
BF16 = jnp.bfloat16
ANY = pl.BlockSpec(memory_space=pl.ANY)
SMEM = pl.BlockSpec(memory_space=pltpu.SMEM)


def run_copies(pairs, sems):
    copies = [pltpu.make_async_copy(a, b, sems.at[i]) for i, (a, b) in enumerate(pairs)]
    for copy in copies:
        copy.start()
    for copy in copies:
        copy.wait()


def head_columns(chip, heads, r, core):
    return pl.ds(pl.multiple_of((chip * heads + CORES * r + core) * HEAD_DIM, HEAD_DIM), HEAD_DIM)


def give_kernel(n, heads, rounds, place, *refs):
    tensors, out, sems = refs[:6], refs[6], refs[7]
    x, c = place[2], place[3]
    pairs = []
    for i, r in enumerate(rounds):
        for k in range(n):
            at = head_columns(lax.rem(x + k, n), heads, r, 1 - c)
            pairs += [(tensors[t].at[:, at], out.at[i, k, t]) for t in range(6)]
    run_copies(pairs, sems)


def give(place, tensors, n, heads, rounds):
    rows = tensors[0].shape[0]
    return pl.pallas_call(
        functools.partial(give_kernel, n, heads, rounds),
        in_specs=[SMEM] + [ANY] * 6,
        out_specs=ANY,
        out_shape=jax.ShapeDtypeStruct((len(rounds), n, 6, rows, HEAD_DIM), BF16),
        scratch_shapes=[pltpu.SemaphoreType.DMA((6 * n * len(rounds),))],
        name="give",
    )(place, *tensors)


def merge_kernel(n, heads, r, i, place, *refs):
    tensors, got, outs, sems = refs[:6], refs[6], refs[7 : 7 + n], refs[7 + n]
    x, c = place[2], place[3]
    rows = got.shape[-2]
    own = pl.ds(pl.multiple_of(c * rows, rows), rows)
    others = pl.ds(pl.multiple_of((1 - c) * rows, rows), rows)
    pairs = []
    for k in [*range(1, n), 0]:
        at = head_columns(lax.rem(x + k, n), heads, r, c)
        pairs += [(tensors[t].at[:, at], outs[k].at[t, own]) for t in range(6)]
        pairs += [(got.at[i, k], outs[k].at[:, others])]
    run_copies(pairs, sems)


def merge(place, tensors, got, n, heads, r, i):
    rows = tensors[0].shape[0]
    return pl.pallas_call(
        functools.partial(merge_kernel, n, heads, r, i),
        in_specs=[SMEM] + [ANY] * 7,
        out_specs=[ANY] * n,
        out_shape=[jax.ShapeDtypeStruct((6, CORES * rows, HEAD_DIM), BF16)] * n,
        scratch_shapes=[pltpu.SemaphoreType.DMA((7 * n,))],
        name="merge",
    )(place, *tensors, got)


def nt_dot(a, b):
    return lax.dot_general(a, b, (((1,), (1,)), ((), ())), preferred_element_type=jnp.float32)


def attend_kernel(n, info, *refs):
    moved, outs, (qq, kk, vv, held, sems) = refs[:n], refs[n : 2 * n], refs[2 * n :]
    rows = moved[0].shape[1]
    per = rows // FRAME
    x = info[2]
    idle = x >= n
    first_count = jnp.where(idle, 0, info[0])
    second_count = jnp.where(idle, 0, info[1])
    used = first_count + second_count
    factor = LOG2E / math.sqrt(HEAD_DIM)
    scale = 1.0 / math.sqrt(HEAD_DIM)

    pairs = []
    for k in range(n):
        at = pl.ds(pl.multiple_of(lax.rem(x + n - k, n) * rows, rows), rows)
        for t, (ref, half) in enumerate(((qq, 1), (kk, 0), (vv, 0), (qq, 0), (kk, 1), (vv, 1))):
            pairs.append((moved[k].at[t], ref.at[at, half * HEAD_DIM : (half + 1) * HEAD_DIM]))
    run_copies(pairs, sems)

    def store(frame, which, value):
        at = pl.multiple_of(lax.rem(frame, per) * FRAME, FRAME)
        held[lax.div(frame, per), which, pl.ds(at, FRAME), :] = value

    def one_video(start, count):
        keys = pl.ds(pl.multiple_of(start * FRAME, FRAME), count * FRAME)

        def one_frame(i, carry):
            frame = start + i
            at = pl.ds(pl.multiple_of(frame * FRAME, FRAME), FRAME)
            s = nt_dot(qq[at, HEAD_DIM:], kk[keys, :HEAD_DIM]) * factor
            t = nt_dot(qq[at, :], kk[keys, :]) * scale
            e = jnp.exp2(s - jnp.max(s, axis=1, keepdims=True))
            p = e * (1.0 / jnp.sum(e, axis=1, keepdims=True))
            mean = jnp.sum(p * t, axis=1, keepdims=True)
            low = p.astype(BF16)
            turned = (p * (t - mean)).astype(BF16)
            both = jnp.dot(low, vv[keys, :], preferred_element_type=jnp.float32)
            more = jnp.dot(turned, vv[keys, :HEAD_DIM], preferred_element_type=jnp.float32)
            store(frame, 0, both[:, :HEAD_DIM].astype(BF16))
            store(frame, 1, (both[:, HEAD_DIM:] + more).astype(BF16))
            return carry

        lax.fori_loop(0, count, one_frame, 0)

    def video(i, carry):
        start = jnp.where(i == 0, 0, first_count)
        count = jnp.where(i == 0, first_count, second_count)
        for frames in range(1, FRAMES_MOST + 1):
            pl.when(count == frames)(functools.partial(one_video, start, frames))
        return carry

    lax.fori_loop(0, 2, video, 0)

    def blank(frame, carry):
        nothing = jnp.zeros((FRAME, HEAD_DIM), BF16)
        store(frame, 0, nothing)
        store(frame, 1, nothing)
        return carry

    lax.fori_loop(used, n * per, blank, 0)
    for k in range(n):
        outs[k][...] = held[lax.rem(x + k, n)]


def attend(info, moved):
    n = len(moved)
    rows = moved[0].shape[1]
    return pl.pallas_call(
        functools.partial(attend_kernel, n),
        in_specs=[SMEM] + [ANY] * n,
        out_specs=[pl.BlockSpec(memory_space=pltpu.VMEM)] * n,
        out_shape=[jax.ShapeDtypeStruct((2, rows, HEAD_DIM), BF16)] * n,
        scratch_shapes=[pltpu.VMEM((n * rows, 2 * HEAD_DIM), BF16)] * 3
        + [pltpu.VMEM((n, 2, rows, HEAD_DIM), BF16), pltpu.SemaphoreType.DMA((6 * n,))],
        compiler_params=pltpu.CompilerParams(vmem_limit_bytes=40 * 2**20),
        cost_estimate=pl.CostEstimate(
            flops=5 * 10**9, bytes_accessed=4 * 2**20, transcendentals=2**21
        ),
        name="attend",
    )(info, *moved)


def project_kernel(n, heads, sizes, place, *refs):
    groups = len(sizes)
    mine, others = refs[: groups * n], refs[groups * n : groups * (n + 1)]
    w_own, w_other, out, tangent, held, sems = refs[groups * (n + 1) :]
    x, c = place[2], place[3]
    rows = out.shape[0]
    step = pl.program_id(0)
    half = pl.num_programs(0) // 2

    @pl.when(step == 0)
    def _():
        own = pl.ds(pl.multiple_of(c * rows, rows), rows)
        pairs, r = [], 0
        for g, size in enumerate(sizes):
            for i in range(size):
                for k in range(n):
                    chip = lax.rem(x + n - k, n)
                    for which in range(2):
                        down = slice(which * rows, (which + 1) * rows)
                        at = head_columns(chip, heads, r, c)
                        pairs.append((mine[g * n + k].at[i, which, own], held.at[down, at]))
                        at = head_columns(chip, heads, r, 1 - c)
                        pairs.append((others[g].at[i, k, which], held.at[down, at]))
                r += 1
        run_copies(pairs, sems)

    @pl.when(x >= n)
    def _():
        out[...] = jnp.zeros_like(out)
        tangent[...] = jnp.zeros_like(tangent)

    def finish(w):
        product = jnp.dot(held[...], w[...], preferred_element_type=jnp.float32)
        out[...] = product[:rows].astype(BF16)
        tangent[...] = product[rows:].astype(BF16)

    pl.when((x < n) & (step < half))(lambda: finish(w_own))
    pl.when((x < n) & (step >= half))(lambda: finish(w_other))


def project(place, mine, others, w_own, w_other, n, heads):
    sizes = tuple(o.shape[0] for o in others)
    rows = others[0].shape[3]
    depth, width = w_own.shape
    tile = 512
    half = width // tile

    def at(step, place):
        return (0, jnp.where(step < half, place[3] * half + step, (1 - place[3]) * half + step - half))

    given = pl.BlockSpec((rows, tile), at)
    return pl.pallas_call(
        functools.partial(project_kernel, n, heads, sizes),
        grid_spec=pltpu.PrefetchScalarGridSpec(
            num_scalar_prefetch=1,
            grid=(2 * half,),
            in_specs=[ANY] * (len(sizes) * (n + 1))
            + [
                pl.BlockSpec((depth, tile), lambda step, place: (0, jnp.minimum(step, half - 1))),
                pl.BlockSpec((depth, tile), lambda step, place: (0, jnp.maximum(step - half, 0))),
            ],
            out_specs=[given, given],
            scratch_shapes=[
                pltpu.VMEM((2 * rows, depth), BF16),
                pltpu.SemaphoreType.DMA((4 * n * sum(sizes),)),
            ],
        ),
        out_shape=[jax.ShapeDtypeStruct((rows, CORES * width), BF16)] * 2,
        compiler_params=pltpu.CompilerParams(vmem_limit_bytes=48 * 2**20),
        name="project",
    )(place, *[m for group in mine for m in group], *others, w_own, w_other)


def after(value, *done):
    return lax.optimization_barrier((value, done))[0]


def hop(value, chips):
    pairs = [(a * CORES + c, b * CORES + c) for a, b in chips for c in range(CORES)]
    return lax.ppermute(value, "ulysses", pairs)


def swap(value):
    members = lax.axis_size("ulysses")
    return lax.ppermute(value, "ulysses", [(u, u ^ 1) for u in range(members)])


def turn(blocks, line, x, parts=1):
    n = len(blocks) + 1
    if n == line:
        return [hop(b, [(i, (i + k) % n) for i in range(n)]) for k, b in enumerate(blocks, 1)]
    up, down = blocks
    came_up = hop(up, [(i, (i + 1) % n) for i in range(n)])
    pieces = []
    for piece in jnp.split(down, parts):
        first = hop(piece, [(1, 0), (2, 1), (0, 3)])
        second = hop(first, [(3, 2)])
        pieces.append(jnp.where(x == 2, second, first))
    return [came_up, jnp.concatenate(pieces) if parts > 1 else pieces[0]]


def gather_weight(out_weight, core):
    members = lax.axis_size("ulysses")
    left, right = jnp.split(out_weight, 2, axis=1)
    got = swap(jnp.where(core == 0, right, left))
    kept = jnp.where(core == 0, left, right)
    rows = jnp.concatenate([jnp.where(core == 0, kept, got), jnp.where(core == 0, got, kept)])
    same_core = [[u for u in range(members) if u % CORES == c] for c in range(CORES)]
    rows = lax.all_gather(rows, "ulysses", axis_index_groups=same_core, axis=0, tiled=True)
    own = lax.all_gather(rows, "dp", axis=0, tiled=True)
    return own, swap(own)


def run(n, line, place, out_weight, *tensors):
    heads = tensors[0].shape[1] // HEAD_DIM // n
    rounds = heads // CORES
    x, c = place[2], place[3]
    w_own, w_other = gather_weight(out_weight, c)
    got_first = swap(give(place, tensors, n, heads, (0,)))
    got_rest = swap(give(place, tensors, n, heads, tuple(range(1, rounds))))
    arrived, results = [], []
    for r in range(rounds):
        got, i = (got_first, 0) if r == 0 else (got_rest, r - 1)
        kept, *sent = merge(place, tensors, got, n, heads, r, i)
        if r >= 2:
            sent = list(after(tuple(sent), arrived[r - 2]))
        came = turn(sent, line, x, parts=2 if r == rounds - 1 else 1)
        arrived.append(tuple(came))
        results.append(attend(place, [kept, *came]))
    mine, others = [], []
    for group in (results[:-1], results[-1:]):
        kept, *sent = [jnp.stack([r[k] for r in group]) for k in range(n)]
        whole = [kept, *turn(sent, line, x)]
        rows = tensors[0].shape[0]
        theirs = [lax.dynamic_slice_in_dim(t, (1 - c) * rows, rows, 2) for t in whole]
        mine.append(whole)
        others.append(swap(jnp.stack(theirs, axis=1)))
    return tuple(project(place, mine, others, w_own, w_other, n, heads))


def shards(q, k, v, dq, dk, dv, out_weight, frame_counts, token_offsets, video_group):
    members, groups = lax.axis_size("ulysses"), lax.axis_size("dp")
    line = members // CORES
    per_chip = CORES * q.shape[0] // FRAME
    u = lax.axis_index("ulysses")
    mine = video_group == lax.axis_index("dp")
    place = jnp.stack(
        [
            jnp.sum(jnp.where(mine & (token_offsets == 0), frame_counts, 0)),
            jnp.sum(jnp.where(mine & (token_offsets > 0), frame_counts, 0)),
            u // CORES,
            u % CORES,
        ]
    ).astype(jnp.int32)
    in_group = video_group[None, :] == jnp.arange(groups, dtype=video_group.dtype)[:, None]
    most = jnp.max(jnp.sum(jnp.where(in_group, frame_counts[None, :], 0), axis=1))
    return lax.cond(
        most <= (line - 1) * per_chip,
        functools.partial(run, line - 1, line),
        functools.partial(run, line, line),
        place,
        out_weight,
        q,
        k,
        v,
        dq,
        dk,
        dv,
    )


def solution(mesh):
    split = P(("dp", "ulysses"), None)
    return jax.shard_map(
        shards,
        mesh=mesh,
        in_specs=(split,) * 7 + (P(),) * 3,
        out_specs=(split, split),
        check_vma=False,
    )
```

```python
import functools
import math

import jax
import jax.numpy as jnp
from jax import lax
from jax.experimental import pallas as pl
from jax.experimental.pallas import tpu as pltpu
from jax.sharding import PartitionSpec as P

HEAD_DIM = 128
FRAME = 128
FRAMES_MOST = 8
CORES = 2
LOG2E = 1.4426950408889634
BF16 = jnp.bfloat16
ANY = pl.BlockSpec(memory_space=pl.ANY)
SMEM = pl.BlockSpec(memory_space=pltpu.SMEM)
VMEM = pl.BlockSpec(memory_space=pltpu.VMEM)


def run_copies(pairs, sems):
    copies = [pltpu.make_async_copy(a, b, sems.at[i]) for i, (a, b) in enumerate(pairs)]
    for copy in copies:
        copy.start()
    for copy in copies:
        copy.wait()


def head_columns(chip, heads, r, core):
    return pl.ds(pl.multiple_of((chip * heads + CORES * r + core) * HEAD_DIM, HEAD_DIM), HEAD_DIM)


def give_kernel(n, heads, rounds, place, *refs):
    tensors, out, sems = refs[:6], refs[6], refs[7]
    x, c = place[2], place[3]
    pairs = []
    for i, r in enumerate(rounds):
        for k in range(n):
            at = head_columns(lax.rem(x + k, n), heads, r, 1 - c)
            pairs += [(tensors[t].at[:, at], out.at[i, k, t]) for t in range(6)]
    run_copies(pairs, sems)


def give(place, tensors, n, heads, rounds):
    rows = tensors[0].shape[0]
    return pl.pallas_call(
        functools.partial(give_kernel, n, heads, rounds),
        in_specs=[SMEM] + [ANY] * 6,
        out_specs=VMEM,
        out_shape=jax.ShapeDtypeStruct((len(rounds), n, 6, rows, HEAD_DIM), BF16),
        scratch_shapes=[pltpu.SemaphoreType.DMA((6 * n * len(rounds),))],
        name="give",
    )(place, *tensors)


def merge_kernel(n, heads, r, i, place, *refs):
    tensors, got, outs, sems = refs[:6], refs[6], refs[7 : 7 + n], refs[7 + n]
    x, c = place[2], place[3]
    rows = got.shape[-2]
    own = pl.ds(pl.multiple_of(c * rows, rows), rows)
    others = pl.ds(pl.multiple_of((1 - c) * rows, rows), rows)
    pairs = []
    for k in [*range(1, n), 0]:
        at = head_columns(lax.rem(x + k, n), heads, r, c)
        pairs += [(tensors[t].at[:, at], outs[k].at[t, own]) for t in range(6)]
        pairs += [(got.at[i, k], outs[k].at[:, others])]
    run_copies(pairs, sems)


def merge(place, tensors, got, n, heads, r, i):
    rows = tensors[0].shape[0]
    return pl.pallas_call(
        functools.partial(merge_kernel, n, heads, r, i),
        in_specs=[SMEM] + [ANY] * 7,
        out_specs=[VMEM] * n,
        out_shape=[jax.ShapeDtypeStruct((6, CORES * rows, HEAD_DIM), BF16)] * n,
        scratch_shapes=[pltpu.SemaphoreType.DMA((7 * n,))],
        name="merge",
    )(place, *tensors, got)


def nt_dot(a, b):
    return lax.dot_general(a, b, (((1,), (1,)), ((), ())), preferred_element_type=jnp.float32)


def attend_kernel(n, info, *refs):
    moved, outs, (qq, kk, vv, held, sems) = refs[:n], refs[n : 2 * n], refs[2 * n :]
    rows = moved[0].shape[1]
    per = rows // FRAME
    x = info[2]
    idle = x >= n
    first_count = jnp.where(idle, 0, info[0])
    second_count = jnp.where(idle, 0, info[1])
    used = first_count + second_count
    factor = LOG2E / math.sqrt(HEAD_DIM)
    scale = 1.0 / math.sqrt(HEAD_DIM)

    pairs = []
    for k in range(n):
        at = pl.ds(pl.multiple_of(lax.rem(x + n - k, n) * rows, rows), rows)
        for t, (ref, half) in enumerate(((qq, 1), (kk, 0), (vv, 0), (qq, 0), (kk, 1), (vv, 1))):
            pairs.append((moved[k].at[t], ref.at[at, half * HEAD_DIM : (half + 1) * HEAD_DIM]))
    run_copies(pairs, sems)

    def store(frame, which, value):
        at = pl.multiple_of(lax.rem(frame, per) * FRAME, FRAME)
        held[lax.div(frame, per), which, pl.ds(at, FRAME), :] = value

    def one_video(start, count):
        keys = pl.ds(pl.multiple_of(start * FRAME, FRAME), count * FRAME)

        def one_frame(i, carry):
            frame = start + i
            at = pl.ds(pl.multiple_of(frame * FRAME, FRAME), FRAME)
            s = nt_dot(qq[at, HEAD_DIM:], kk[keys, :HEAD_DIM]) * factor
            t = nt_dot(qq[at, :], kk[keys, :]) * scale
            e = jnp.exp2(s - jnp.max(s, axis=1, keepdims=True))
            p = e * (1.0 / jnp.sum(e, axis=1, keepdims=True))
            mean = jnp.sum(p * t, axis=1, keepdims=True)
            low = p.astype(BF16)
            turned = (p * (t - mean)).astype(BF16)
            both = jnp.dot(low, vv[keys, :], preferred_element_type=jnp.float32)
            more = jnp.dot(turned, vv[keys, :HEAD_DIM], preferred_element_type=jnp.float32)
            store(frame, 0, both[:, :HEAD_DIM].astype(BF16))
            store(frame, 1, (both[:, HEAD_DIM:] + more).astype(BF16))
            return carry

        lax.fori_loop(0, count, one_frame, 0)

    def video(i, carry):
        start = jnp.where(i == 0, 0, first_count)
        count = jnp.where(i == 0, first_count, second_count)
        for frames in range(1, FRAMES_MOST + 1):
            pl.when(count == frames)(functools.partial(one_video, start, frames))
        return carry

    lax.fori_loop(0, 2, video, 0)

    def blank(frame, carry):
        nothing = jnp.zeros((FRAME, HEAD_DIM), BF16)
        store(frame, 0, nothing)
        store(frame, 1, nothing)
        return carry

    lax.fori_loop(used, n * per, blank, 0)
    for k in range(n):
        outs[k][...] = held[lax.rem(x + k, n)]


def attend(info, moved):
    n = len(moved)
    rows = moved[0].shape[1]
    return pl.pallas_call(
        functools.partial(attend_kernel, n),
        in_specs=[SMEM] + [ANY] * n,
        out_specs=[VMEM] * n,
        out_shape=[jax.ShapeDtypeStruct((2, rows, HEAD_DIM), BF16)] * n,
        scratch_shapes=[pltpu.VMEM((n * rows, 2 * HEAD_DIM), BF16)] * 3
        + [pltpu.VMEM((n, 2, rows, HEAD_DIM), BF16), pltpu.SemaphoreType.DMA((6 * n,))],
        compiler_params=pltpu.CompilerParams(vmem_limit_bytes=40 * 2**20),
        cost_estimate=pl.CostEstimate(
            flops=5 * 10**9, bytes_accessed=4 * 2**20, transcendentals=2**21
        ),
        name="attend",
    )(info, *moved)


def project_kernel(n, heads, sizes, place, *refs):
    groups = len(sizes)
    mine, others = refs[: groups * n], refs[groups * n : groups * (n + 1)]
    w_own, w_other, out, tangent, held, sems = refs[groups * (n + 1) :]
    x, c = place[2], place[3]
    rows = out.shape[0]
    step = pl.program_id(0)
    half = pl.num_programs(0) // 2

    @pl.when(step == 0)
    def _():
        own = pl.ds(pl.multiple_of(c * rows, rows), rows)
        pairs, r = [], 0
        for g, size in enumerate(sizes):
            for i in range(size):
                for k in range(n):
                    chip = lax.rem(x + n - k, n)
                    for which in range(2):
                        down = slice(which * rows, (which + 1) * rows)
                        at = head_columns(chip, heads, r, c)
                        pairs.append((mine[g * n + k].at[i, which, own], held.at[down, at]))
                        at = head_columns(chip, heads, r, 1 - c)
                        pairs.append((others[g].at[i, k, which], held.at[down, at]))
                r += 1
        run_copies(pairs, sems)

    @pl.when(x >= n)
    def _():
        out[...] = jnp.zeros_like(out)
        tangent[...] = jnp.zeros_like(tangent)

    def finish(w):
        product = jnp.dot(held[...], w[...], preferred_element_type=jnp.float32)
        out[...] = product[:rows].astype(BF16)
        tangent[...] = product[rows:].astype(BF16)

    pl.when((x < n) & (step < half))(lambda: finish(w_own))
    pl.when((x < n) & (step >= half))(lambda: finish(w_other))


def project(place, mine, others, w_own, w_other, n, heads):
    sizes = tuple(o.shape[0] for o in others)
    rows = others[0].shape[3]
    depth, width = w_own.shape
    tile = 512
    half = width // tile

    def at(step, place):
        return (0, jnp.where(step < half, place[3] * half + step, (1 - place[3]) * half + step - half))

    given = pl.BlockSpec((rows, tile), at)
    return pl.pallas_call(
        functools.partial(project_kernel, n, heads, sizes),
        grid_spec=pltpu.PrefetchScalarGridSpec(
            num_scalar_prefetch=1,
            grid=(2 * half,),
            in_specs=[ANY] * (len(sizes) * (n + 1))
            + [
                pl.BlockSpec((depth, tile), lambda step, place: (0, jnp.minimum(step, half - 1))),
                pl.BlockSpec((depth, tile), lambda step, place: (0, jnp.maximum(step - half, 0))),
            ],
            out_specs=[given, given],
            scratch_shapes=[
                pltpu.VMEM((2 * rows, depth), BF16),
                pltpu.SemaphoreType.DMA((4 * n * sum(sizes),)),
            ],
        ),
        out_shape=[jax.ShapeDtypeStruct((rows, CORES * width), BF16)] * 2,
        compiler_params=pltpu.CompilerParams(vmem_limit_bytes=48 * 2**20),
        name="project",
    )(place, *[m for group in mine for m in group], *others, w_own, w_other)


def after(value, *done):
    return lax.optimization_barrier((value, done))[0]


def hop(value, chips):
    pairs = [(a * CORES + c, b * CORES + c) for a, b in chips for c in range(CORES)]
    return lax.ppermute(value, "ulysses", pairs)


def swap(value):
    members = lax.axis_size("ulysses")
    return lax.ppermute(value, "ulysses", [(u, u ^ 1) for u in range(members)])


def turn(blocks, line, x, parts=1):
    n = len(blocks) + 1
    if n == line:
        return [hop(b, [(i, (i + k) % n) for i in range(n)]) for k, b in enumerate(blocks, 1)]
    up, down = blocks
    came_up = hop(up, [(i, (i + 1) % n) for i in range(n)])
    pieces = []
    for piece in jnp.split(down, parts):
        first = hop(piece, [(1, 0), (2, 1), (0, 3)])
        second = hop(first, [(3, 2)])
        pieces.append(jnp.where(x == 2, second, first))
    return [came_up, jnp.concatenate(pieces) if parts > 1 else pieces[0]]


def gather_weight(out_weight, core):
    members = lax.axis_size("ulysses")
    left, right = jnp.split(out_weight, 2, axis=1)
    got = swap(jnp.where(core == 0, right, left))
    kept = jnp.where(core == 0, left, right)
    rows = jnp.concatenate([jnp.where(core == 0, kept, got), jnp.where(core == 0, got, kept)])
    same_core = [[u for u in range(members) if u % CORES == c] for c in range(CORES)]
    rows = lax.all_gather(rows, "ulysses", axis_index_groups=same_core, axis=0, tiled=True)
    own = lax.all_gather(rows, "dp", axis=0, tiled=True)
    return own, swap(own)


def run(n, line, place, out_weight, *tensors):
    heads = tensors[0].shape[1] // HEAD_DIM // n
    rounds = heads // CORES
    x, c = place[2], place[3]
    w_own, w_other = gather_weight(out_weight, c)
    got_first = swap(give(place, tensors, n, heads, (0,)))
    got_rest = swap(give(place, tensors, n, heads, tuple(range(1, rounds))))
    arrived, results = [], []
    for r in range(rounds):
        got, i = (got_first, 0) if r == 0 else (got_rest, r - 1)
        kept, *sent = merge(place, tensors, got, n, heads, r, i)
        if r >= 2:
            sent = list(after(tuple(sent), arrived[r - 2]))
        came = turn(sent, line, x, parts=2 if r == rounds - 1 else 1)
        arrived.append(tuple(came))
        results.append(attend(place, [kept, *came]))
    mine, others = [], []
    for group in (results[:-1], results[-1:]):
        kept, *sent = [jnp.stack([r[k] for r in group]) for k in range(n)]
        whole = [kept, *turn(sent, line, x)]
        rows = tensors[0].shape[0]
        theirs = [lax.dynamic_slice_in_dim(t, (1 - c) * rows, rows, 2) for t in whole]
        mine.append(whole)
        others.append(swap(jnp.stack(theirs, axis=1)))
    return tuple(project(place, mine, others, w_own, w_other, n, heads))


def shards(q, k, v, dq, dk, dv, out_weight, frame_counts, token_offsets, video_group):
    members, groups = lax.axis_size("ulysses"), lax.axis_size("dp")
    line = members // CORES
    per_chip = CORES * q.shape[0] // FRAME
    u = lax.axis_index("ulysses")
    mine = video_group == lax.axis_index("dp")
    place = jnp.stack(
        [
            jnp.sum(jnp.where(mine & (token_offsets == 0), frame_counts, 0)),
            jnp.sum(jnp.where(mine & (token_offsets > 0), frame_counts, 0)),
            u // CORES,
            u % CORES,
        ]
    ).astype(jnp.int32)
    in_group = video_group[None, :] == jnp.arange(groups, dtype=video_group.dtype)[:, None]
    most = jnp.max(jnp.sum(jnp.where(in_group, frame_counts[None, :], 0), axis=1))
    return lax.cond(
        most <= (line - 1) * per_chip,
        functools.partial(run, line - 1, line),
        functools.partial(run, line, line),
        place,
        out_weight,
        q,
        k,
        v,
        dq,
        dk,
        dv,
    )


def solution(mesh):
    split = P(("dp", "ulysses"), None)
    return jax.shard_map(
        shards,
        mesh=mesh,
        in_specs=(split,) * 7 + (P(),) * 3,
        out_specs=(split, split),
        check_vma=False,
    )
```

```python
import functools
import math

import jax
import jax.numpy as jnp
from jax import lax
from jax.experimental import pallas as pl
from jax.experimental.pallas import tpu as pltpu
from jax.sharding import PartitionSpec as P

HEAD_DIM = 128
FRAME = 128
FRAMES_MOST = 8
CORES = 2
LOG2E = 1.4426950408889634
BF16 = jnp.bfloat16
ANY = pl.BlockSpec(memory_space=pl.ANY)
SMEM = pl.BlockSpec(memory_space=pltpu.SMEM)
VMEM = pl.BlockSpec(memory_space=pltpu.VMEM)


def run_copies(pairs, sems):
    copies = [pltpu.make_async_copy(a, b, sems.at[i]) for i, (a, b) in enumerate(pairs)]
    for copy in copies:
        copy.start()
    for copy in copies:
        copy.wait()


def head_columns(chip, heads, r, core):
    return pl.ds(pl.multiple_of((chip * heads + CORES * r + core) * HEAD_DIM, HEAD_DIM), HEAD_DIM)


def give_kernel(n, heads, rounds, place, *refs):
    tensors, out, sems = refs[:6], refs[6], refs[7]
    x, c = place[2], place[3]
    pairs = []
    for i, r in enumerate(rounds):
        for k in range(n):
            at = head_columns(lax.rem(x + k, n), heads, r, 1 - c)
            pairs += [(tensors[t].at[:, at], out.at[i, k, t]) for t in range(6)]
    run_copies(pairs, sems)


def give(place, tensors, n, heads, rounds):
    rows = tensors[0].shape[0]
    return pl.pallas_call(
        functools.partial(give_kernel, n, heads, rounds),
        in_specs=[SMEM] + [ANY] * 6,
        out_specs=VMEM,
        out_shape=jax.ShapeDtypeStruct((len(rounds), n, 6, rows, HEAD_DIM), BF16),
        scratch_shapes=[pltpu.SemaphoreType.DMA((6 * n * len(rounds),))],
        name="give",
    )(place, *tensors)


def merge_kernel(n, heads, r, i, place, *refs):
    tensors, got, outs, sems = refs[:6], refs[6], refs[7 : 7 + n], refs[7 + n]
    x, c = place[2], place[3]
    rows = got.shape[-2]
    own = pl.ds(pl.multiple_of(c * rows, rows), rows)
    others = pl.ds(pl.multiple_of((1 - c) * rows, rows), rows)
    pairs = []
    for k in [*range(1, n), 0]:
        at = head_columns(lax.rem(x + k, n), heads, r, c)
        pairs += [(tensors[t].at[:, at], outs[k].at[t, own]) for t in range(6)]
        pairs += [(got.at[i, k], outs[k].at[:, others])]
    run_copies(pairs, sems)


def merge(place, tensors, got, n, heads, r, i):
    rows = tensors[0].shape[0]
    return pl.pallas_call(
        functools.partial(merge_kernel, n, heads, r, i),
        in_specs=[SMEM] + [ANY] * 7,
        out_specs=[VMEM] * n,
        out_shape=[jax.ShapeDtypeStruct((6, CORES * rows, HEAD_DIM), BF16)] * n,
        scratch_shapes=[pltpu.SemaphoreType.DMA((7 * n,))],
        name="merge",
    )(place, *tensors, got)


def nt_dot(a, b):
    return lax.dot_general(a, b, (((1,), (1,)), ((), ())), preferred_element_type=jnp.float32)


def attend_kernel(n, info, *refs):
    moved, outs, (qq, kk, vv, held, sems) = refs[:n], refs[n : 2 * n], refs[2 * n :]
    rows = moved[0].shape[1]
    per = rows // FRAME
    x = info[2]
    idle = x >= n
    first_count = jnp.where(idle, 0, info[0])
    second_count = jnp.where(idle, 0, info[1])
    used = first_count + second_count
    factor = LOG2E / math.sqrt(HEAD_DIM)
    scale = 1.0 / math.sqrt(HEAD_DIM)

    pairs = []
    for k in range(n):
        at = pl.ds(pl.multiple_of(lax.rem(x + n - k, n) * rows, rows), rows)
        for t, (ref, half) in enumerate(((qq, 1), (kk, 0), (vv, 0), (qq, 0), (kk, 1), (vv, 1))):
            pairs.append((moved[k].at[t], ref.at[at, half * HEAD_DIM : (half + 1) * HEAD_DIM]))
    run_copies(pairs, sems)

    def store(frame, which, value):
        at = pl.multiple_of(lax.rem(frame, per) * FRAME, FRAME)
        held[lax.div(frame, per), which, pl.ds(at, FRAME), :] = value

    def one_video(start, count):
        keys = pl.ds(pl.multiple_of(start * FRAME, FRAME), count * FRAME)

        def one_frame(i, carry):
            frame = start + i
            at = pl.ds(pl.multiple_of(frame * FRAME, FRAME), FRAME)
            s = nt_dot(qq[at, HEAD_DIM:], kk[keys, :HEAD_DIM]) * factor
            t = nt_dot(qq[at, :], kk[keys, :]) * scale
            e = jnp.exp2(s - jnp.max(s, axis=1, keepdims=True))
            p = e * (1.0 / jnp.sum(e, axis=1, keepdims=True))
            mean = jnp.sum(p * t, axis=1, keepdims=True)
            low = p.astype(BF16)
            turned = (p * (t - mean)).astype(BF16)
            both = jnp.dot(low, vv[keys, :], preferred_element_type=jnp.float32)
            more = jnp.dot(turned, vv[keys, :HEAD_DIM], preferred_element_type=jnp.float32)
            store(frame, 0, both[:, :HEAD_DIM].astype(BF16))
            store(frame, 1, (both[:, HEAD_DIM:] + more).astype(BF16))
            return carry

        lax.fori_loop(0, count, one_frame, 0)

    def video(i, carry):
        start = jnp.where(i == 0, 0, first_count)
        count = jnp.where(i == 0, first_count, second_count)
        for frames in range(1, FRAMES_MOST + 1):
            pl.when(count == frames)(functools.partial(one_video, start, frames))
        return carry

    lax.fori_loop(0, 2, video, 0)

    def blank(frame, carry):
        nothing = jnp.zeros((FRAME, HEAD_DIM), BF16)
        store(frame, 0, nothing)
        store(frame, 1, nothing)
        return carry

    lax.fori_loop(used, n * per, blank, 0)
    for k in range(n):
        outs[k][...] = held[lax.rem(x + k, n)]


def attend(info, moved):
    n = len(moved)
    rows = moved[0].shape[1]
    return pl.pallas_call(
        functools.partial(attend_kernel, n),
        in_specs=[SMEM] + [ANY] * n,
        out_specs=[VMEM] * n,
        out_shape=[jax.ShapeDtypeStruct((2, rows, HEAD_DIM), BF16)] * n,
        scratch_shapes=[pltpu.VMEM((n * rows, 2 * HEAD_DIM), BF16)] * 3
        + [pltpu.VMEM((n, 2, rows, HEAD_DIM), BF16), pltpu.SemaphoreType.DMA((6 * n,))],
        compiler_params=pltpu.CompilerParams(vmem_limit_bytes=40 * 2**20),
        cost_estimate=pl.CostEstimate(
            flops=5 * 10**9, bytes_accessed=4 * 2**20, transcendentals=2**21
        ),
        name="attend",
    )(info, *moved)


def project_kernel(n, heads, sizes, place, *refs):
    groups = len(sizes)
    mine, others = refs[: groups * n], refs[groups * n : groups * (n + 1)]
    w_own, w_other, out, tangent, held, sems = refs[groups * (n + 1) :]
    x, c = place[2], place[3]
    rows = out.shape[0]
    step = pl.program_id(0)
    half = pl.num_programs(0) // 2

    @pl.when(step == 0)
    def _():
        own = pl.ds(pl.multiple_of(c * rows, rows), rows)
        pairs, r = [], 0
        for g, size in enumerate(sizes):
            for i in range(size):
                for k in range(n):
                    chip = lax.rem(x + n - k, n)
                    for which in range(2):
                        down = slice(which * rows, (which + 1) * rows)
                        at = head_columns(chip, heads, r, c)
                        pairs.append((mine[g * n + k].at[i, which, own], held.at[down, at]))
                        at = head_columns(chip, heads, r, 1 - c)
                        pairs.append((others[g].at[i, k, which], held.at[down, at]))
                r += 1
        run_copies(pairs, sems)

    @pl.when(x >= n)
    def _():
        out[...] = jnp.zeros_like(out)
        tangent[...] = jnp.zeros_like(tangent)

    def finish(w):
        product = jnp.dot(held[...], w[...], preferred_element_type=jnp.float32)
        out[...] = product[:rows].astype(BF16)
        tangent[...] = product[rows:].astype(BF16)

    pl.when((x < n) & (step < half))(lambda: finish(w_own))
    pl.when((x < n) & (step >= half))(lambda: finish(w_other))


def project(place, mine, others, w_own, w_other, n, heads):
    sizes = tuple(o.shape[0] for o in others)
    rows = others[0].shape[3]
    depth, width = w_own.shape
    tile = 512
    half = width // tile

    def at(step, place):
        return (0, jnp.where(step < half, place[3] * half + step, (1 - place[3]) * half + step - half))

    given = pl.BlockSpec((rows, tile), at)
    return pl.pallas_call(
        functools.partial(project_kernel, n, heads, sizes),
        grid_spec=pltpu.PrefetchScalarGridSpec(
            num_scalar_prefetch=1,
            grid=(2 * half,),
            in_specs=[ANY] * (len(sizes) * (n + 1))
            + [
                pl.BlockSpec((depth, tile), lambda step, place: (0, jnp.minimum(step, half - 1))),
                pl.BlockSpec((depth, tile), lambda step, place: (0, jnp.maximum(step - half, 0))),
            ],
            out_specs=[given, given],
            scratch_shapes=[
                pltpu.VMEM((2 * rows, depth), BF16),
                pltpu.SemaphoreType.DMA((4 * n * sum(sizes),)),
            ],
        ),
        out_shape=[jax.ShapeDtypeStruct((rows, CORES * width), BF16)] * 2,
        compiler_params=pltpu.CompilerParams(vmem_limit_bytes=48 * 2**20),
        name="project",
    )(place, *[m for group in mine for m in group], *others, w_own, w_other)


def after(value, *done):
    return lax.optimization_barrier((value, done))[0]


def hop(value, chips):
    pairs = [(a * CORES + c, b * CORES + c) for a, b in chips for c in range(CORES)]
    return lax.ppermute(value, "ulysses", pairs)


def swap(value):
    members = lax.axis_size("ulysses")
    return lax.ppermute(value, "ulysses", [(u, u ^ 1) for u in range(members)])


def turn(blocks, line, x, parts=1):
    n = len(blocks) + 1
    if n == line:
        return [hop(b, [(i, (i + k) % n) for i in range(n)]) for k, b in enumerate(blocks, 1)]
    up, down = blocks
    came_up = hop(up, [(i, (i + 1) % n) for i in range(n)])
    pieces = []
    for piece in jnp.split(down, parts):
        first = hop(piece, [(1, 0), (2, 1), (0, 3)])
        second = hop(first, [(3, 2)])
        pieces.append(jnp.where(x == 2, second, first))
    return [came_up, jnp.concatenate(pieces) if parts > 1 else pieces[0]]


def gather_weight(out_weight, x, core, line):
    left, right = jnp.split(out_weight, 2, axis=1)
    got = swap(jnp.where(core == 0, right, left))
    kept = jnp.where(core == 0, left, right)
    rows = jnp.concatenate([jnp.where(core == 0, kept, got), jnp.where(core == 0, got, kept)])
    back = [hop(rows, [(i, (i + k) % line) for i in range(line)]) for k in range(line - 1, 0, -1)]
    ring = jnp.stack([*back, rows] * 2)
    ordered = lax.dynamic_slice_in_dim(ring, line - 1 - x, line, 0)
    return lax.all_gather(ordered.reshape(-1, rows.shape[1]), "dp", axis=0, tiled=True)


def run(n, line, place, out_weight, *tensors):
    heads = tensors[0].shape[1] // HEAD_DIM // n
    rounds = heads // CORES
    x, c = place[2], place[3]
    got_first = swap(give(place, tensors, n, heads, (0,)))
    w_own = gather_weight(out_weight, x, c, line)
    arrived, results, got_rest, w_other = [], [], None, None
    for r in range(rounds):
        got, i = (got_first, 0) if r == 0 else (got_rest, r - 1)
        kept, *sent = merge(place, tensors, got, n, heads, r, i)
        if r == 0:
            later = after(place, kept)
            got_rest = swap(give(later, tensors, n, heads, tuple(range(1, rounds))))
        if r >= 2:
            sent = list(after(tuple(sent), arrived[r - 2]))
        came = turn(sent, line, x, parts=2 if r == rounds - 1 else 1)
        arrived.append(tuple(came))
        results.append(attend(place, [kept, *came]))
    w_other = swap(after(w_own, arrived[-2]))
    mine, others = [], []
    for group in (results[:-1], results[-1:]):
        kept, *sent = [jnp.stack([r[k] for r in group]) for k in range(n)]
        whole = [kept, *turn(sent, line, x)]
        rows = tensors[0].shape[0]
        theirs = [lax.dynamic_slice_in_dim(t, (1 - c) * rows, rows, 2) for t in whole]
        mine.append(whole)
        others.append(swap(jnp.stack(theirs, axis=1)))
    return tuple(project(place, mine, others, w_own, w_other, n, heads))


def shards(q, k, v, dq, dk, dv, out_weight, frame_counts, token_offsets, video_group):
    members, groups = lax.axis_size("ulysses"), lax.axis_size("dp")
    line = members // CORES
    per_chip = CORES * q.shape[0] // FRAME
    u = lax.axis_index("ulysses")
    mine = video_group == lax.axis_index("dp")
    place = jnp.stack(
        [
            jnp.sum(jnp.where(mine & (token_offsets == 0), frame_counts, 0)),
            jnp.sum(jnp.where(mine & (token_offsets > 0), frame_counts, 0)),
            u // CORES,
            u % CORES,
        ]
    ).astype(jnp.int32)
    in_group = video_group[None, :] == jnp.arange(groups, dtype=video_group.dtype)[:, None]
    most = jnp.max(jnp.sum(jnp.where(in_group, frame_counts[None, :], 0), axis=1))
    return lax.cond(
        most <= (line - 1) * per_chip,
        functools.partial(run, line - 1, line),
        functools.partial(run, line, line),
        place,
        out_weight,
        q,
        k,
        v,
        dq,
        dk,
        dv,
    )


def solution(mesh):
    split = P(("dp", "ulysses"), None)
    return jax.shard_map(
        shards,
        mesh=mesh,
        in_specs=(split,) * 7 + (P(),) * 3,
        out_specs=(split, split),
        check_vma=False,
    )
```

```python
import functools
import math

import jax
import jax.numpy as jnp
from jax import lax
from jax.experimental import pallas as pl
from jax.experimental.pallas import tpu as pltpu
from jax.sharding import PartitionSpec as P

HEAD_DIM = 128
FRAME = 128
FRAMES_MOST = 8
CORES = 2
LOG2E = 1.4426950408889634
BF16 = jnp.bfloat16
ANY = pl.BlockSpec(memory_space=pl.ANY)
SMEM = pl.BlockSpec(memory_space=pltpu.SMEM)
VMEM = pl.BlockSpec(memory_space=pltpu.VMEM)


def run_copies(pairs, sems):
    copies = [pltpu.make_async_copy(a, b, sems.at[i]) for i, (a, b) in enumerate(pairs)]
    for copy in copies:
        copy.start()
    for copy in copies:
        copy.wait()


def head_columns(chip, heads, r, core):
    return pl.ds(pl.multiple_of((chip * heads + CORES * r + core) * HEAD_DIM, HEAD_DIM), HEAD_DIM)


def give_kernel(n, heads, rounds, place, *refs):
    tensors, out, sems = refs[:6], refs[6], refs[7]
    x, c = place[2], place[3]
    pairs = []
    for i, r in enumerate(rounds):
        for k in range(n):
            at = head_columns(lax.rem(x + k, n), heads, r, 1 - c)
            pairs += [(tensors[t].at[:, at], out.at[i, k, t]) for t in range(6)]
    run_copies(pairs, sems)


def give(place, tensors, n, heads, rounds):
    rows = tensors[0].shape[0]
    return pl.pallas_call(
        functools.partial(give_kernel, n, heads, rounds),
        in_specs=[SMEM] + [ANY] * 6,
        out_specs=VMEM,
        out_shape=jax.ShapeDtypeStruct((len(rounds), n, 6, rows, HEAD_DIM), BF16),
        scratch_shapes=[pltpu.SemaphoreType.DMA((6 * n * len(rounds),))],
        name="give",
    )(place, *tensors)


def keep_kernel(n, heads, r, place, *refs):
    tensors, outs, sems = refs[:6], refs[6 : 6 + n], refs[6 + n]
    x, c = place[2], place[3]
    pairs = []
    for k in [*range(1, n), 0]:
        at = head_columns(lax.rem(x + k, n), heads, r, c)
        pairs += [(tensors[t].at[:, at], outs[k].at[t]) for t in range(6)]
    run_copies(pairs, sems)


def keep(place, tensors, n, heads, r):
    rows = tensors[0].shape[0]
    return pl.pallas_call(
        functools.partial(keep_kernel, n, heads, r),
        in_specs=[SMEM] + [ANY] * 6,
        out_specs=[VMEM] * n,
        out_shape=[jax.ShapeDtypeStruct((6, rows, HEAD_DIM), BF16)] * n,
        scratch_shapes=[pltpu.SemaphoreType.DMA((6 * n,))],
        name="keep",
    )(place, *tensors)


def merge_kernel(n, heads, r, i, place, *refs):
    tensors, got, outs, sems = refs[:6], refs[6], refs[7 : 7 + n], refs[7 + n]
    x, c = place[2], place[3]
    rows = got.shape[-2]
    own = pl.ds(pl.multiple_of(c * rows, rows), rows)
    others = pl.ds(pl.multiple_of((1 - c) * rows, rows), rows)
    pairs = []
    for k in [*range(1, n), 0]:
        at = head_columns(lax.rem(x + k, n), heads, r, c)
        pairs += [(tensors[t].at[:, at], outs[k].at[t, own]) for t in range(6)]
        pairs += [(got.at[i, k], outs[k].at[:, others])]
    run_copies(pairs, sems)


def merge(place, tensors, got, n, heads, r, i):
    rows = tensors[0].shape[0]
    return pl.pallas_call(
        functools.partial(merge_kernel, n, heads, r, i),
        in_specs=[SMEM] + [ANY] * 7,
        out_specs=[VMEM] * n,
        out_shape=[jax.ShapeDtypeStruct((6, CORES * rows, HEAD_DIM), BF16)] * n,
        scratch_shapes=[pltpu.SemaphoreType.DMA((7 * n,))],
        name="merge",
    )(place, *tensors, got)


def nt_dot(a, b):
    return lax.dot_general(a, b, (((1,), (1,)), ((), ())), preferred_element_type=jnp.float32)


def attend_kernel(n, kinds, info, *refs):
    size = len(kinds) * n
    moved, outs, (qq, kk, vv, held, sems) = refs[:size], refs[size : size + n], refs[size + n :]
    rows = held.shape[2]
    core_rows = rows // CORES
    per = rows // FRAME
    x, c = info[2], info[3]
    idle = x >= n
    first_count = jnp.where(idle, 0, info[0])
    second_count = jnp.where(idle, 0, info[1])
    used = first_count + second_count
    factor = LOG2E / math.sqrt(HEAD_DIM)
    scale = 1.0 / math.sqrt(HEAD_DIM)

    pairs = []
    for p, kind in enumerate(kinds):
        shift = {"own": c, "other": 1 - c, "both": 0}[kind] * core_rows
        for k in range(n):
            ref = moved[p * n + k]
            base = pl.multiple_of(lax.rem(x + n - k, n) * rows + shift, core_rows)
            at = pl.ds(base, ref.shape[1])
            for t, (to, half) in enumerate(((qq, 1), (kk, 0), (vv, 0), (qq, 0), (kk, 1), (vv, 1))):
                pairs.append((ref.at[t], to.at[at, half * HEAD_DIM : (half + 1) * HEAD_DIM]))
    run_copies(pairs, sems)

    def store(frame, which, value):
        at = pl.multiple_of(lax.rem(frame, per) * FRAME, FRAME)
        held[lax.div(frame, per), which, pl.ds(at, FRAME), :] = value

    def one_video(start, count):
        keys = pl.ds(pl.multiple_of(start * FRAME, FRAME), count * FRAME)

        def one_frame(i, carry):
            frame = start + i
            at = pl.ds(pl.multiple_of(frame * FRAME, FRAME), FRAME)
            s = nt_dot(qq[at, HEAD_DIM:], kk[keys, :HEAD_DIM]) * factor
            t = nt_dot(qq[at, :], kk[keys, :]) * scale
            e = jnp.exp2(s - jnp.max(s, axis=1, keepdims=True))
            p = e * (1.0 / jnp.sum(e, axis=1, keepdims=True))
            mean = jnp.sum(p * t, axis=1, keepdims=True)
            low = p.astype(BF16)
            turned = (p * (t - mean)).astype(BF16)
            both = jnp.dot(low, vv[keys, :], preferred_element_type=jnp.float32)
            more = jnp.dot(turned, vv[keys, :HEAD_DIM], preferred_element_type=jnp.float32)
            store(frame, 0, both[:, :HEAD_DIM].astype(BF16))
            store(frame, 1, (both[:, HEAD_DIM:] + more).astype(BF16))
            return carry

        lax.fori_loop(0, count, one_frame, 0)

    def video(i, carry):
        start = jnp.where(i == 0, 0, first_count)
        count = jnp.where(i == 0, first_count, second_count)
        for frames in range(1, FRAMES_MOST + 1):
            pl.when(count == frames)(functools.partial(one_video, start, frames))
        return carry

    lax.fori_loop(0, 2, video, 0)

    def blank(frame, carry):
        nothing = jnp.zeros((FRAME, HEAD_DIM), BF16)
        store(frame, 0, nothing)
        store(frame, 1, nothing)
        return carry

    lax.fori_loop(used, n * per, blank, 0)
    for k in range(n):
        outs[k][...] = held[lax.rem(x + k, n)]


def attend(info, pieces):
    kinds = tuple(kind for kind, _ in pieces)
    moved = [block for _, blocks in pieces for block in blocks]
    n = len(pieces[0][1])
    rows = sum(blocks[0].shape[1] for _, blocks in pieces)
    return pl.pallas_call(
        functools.partial(attend_kernel, n, kinds),
        in_specs=[SMEM] + [ANY] * len(moved),
        out_specs=[VMEM] * n,
        out_shape=[jax.ShapeDtypeStruct((2, rows, HEAD_DIM), BF16)] * n,
        scratch_shapes=[pltpu.VMEM((n * rows, 2 * HEAD_DIM), BF16)] * 3
        + [pltpu.VMEM((n, 2, rows, HEAD_DIM), BF16), pltpu.SemaphoreType.DMA((6 * len(moved),))],
        compiler_params=pltpu.CompilerParams(vmem_limit_bytes=40 * 2**20),
        cost_estimate=pl.CostEstimate(
            flops=5 * 10**9, bytes_accessed=4 * 2**20, transcendentals=2**21
        ),
        name="attend",
    )(info, *moved)


def project_kernel(n, heads, sizes, place, *refs):
    groups = len(sizes)
    mine, others = refs[: groups * n], refs[groups * n : groups * (n + 1)]
    w_own, w_other, out, tangent, held, sems = refs[groups * (n + 1) :]
    x, c = place[2], place[3]
    rows = out.shape[0]
    step = pl.program_id(0)
    half = pl.num_programs(0) // 2

    @pl.when(step == 0)
    def _():
        own = pl.ds(pl.multiple_of(c * rows, rows), rows)
        pairs, r = [], 0
        for g, size in enumerate(sizes):
            for i in range(size):
                for k in range(n):
                    chip = lax.rem(x + n - k, n)
                    for which in range(2):
                        down = slice(which * rows, (which + 1) * rows)
                        at = head_columns(chip, heads, r, c)
                        pairs.append((mine[g * n + k].at[i, which, own], held.at[down, at]))
                        at = head_columns(chip, heads, r, 1 - c)
                        pairs.append((others[g].at[i, k, which], held.at[down, at]))
                r += 1
        run_copies(pairs, sems)

    @pl.when(x >= n)
    def _():
        out[...] = jnp.zeros_like(out)
        tangent[...] = jnp.zeros_like(tangent)

    def finish(w):
        product = jnp.dot(held[...], w[...], preferred_element_type=jnp.float32)
        out[...] = product[:rows].astype(BF16)
        tangent[...] = product[rows:].astype(BF16)

    pl.when((x < n) & (step < half))(lambda: finish(w_own))
    pl.when((x < n) & (step >= half))(lambda: finish(w_other))


def project(place, mine, others, w_own, w_other, n, heads):
    sizes = tuple(o.shape[0] for o in others)
    rows = others[0].shape[3]
    depth, width = w_own.shape
    tile = 512
    half = width // tile

    def at(step, place):
        return (0, jnp.where(step < half, place[3] * half + step, (1 - place[3]) * half + step - half))

    given = pl.BlockSpec((rows, tile), at)
    return pl.pallas_call(
        functools.partial(project_kernel, n, heads, sizes),
        grid_spec=pltpu.PrefetchScalarGridSpec(
            num_scalar_prefetch=1,
            grid=(2 * half,),
            in_specs=[ANY] * (len(sizes) * (n + 1))
            + [
                pl.BlockSpec((depth, tile), lambda step, place: (0, jnp.minimum(step, half - 1))),
                pl.BlockSpec((depth, tile), lambda step, place: (0, jnp.maximum(step - half, 0))),
            ],
            out_specs=[given, given],
            scratch_shapes=[
                pltpu.VMEM((2 * rows, depth), BF16),
                pltpu.SemaphoreType.DMA((4 * n * sum(sizes),)),
            ],
        ),
        out_shape=[jax.ShapeDtypeStruct((rows, CORES * width), BF16)] * 2,
        compiler_params=pltpu.CompilerParams(vmem_limit_bytes=48 * 2**20),
        name="project",
    )(place, *[m for group in mine for m in group], *others, w_own, w_other)


def after(value, *done):
    return lax.optimization_barrier((value, done))[0]


def hop(value, chips):
    pairs = [(a * CORES + c, b * CORES + c) for a, b in chips for c in range(CORES)]
    return lax.ppermute(value, "ulysses", pairs)


def swap(value):
    members = lax.axis_size("ulysses")
    return lax.ppermute(value, "ulysses", [(u, u ^ 1) for u in range(members)])


def turn(blocks, line, x):
    n = len(blocks) + 1
    if n == line:
        came = [hop(b, [(i, (i + k) % n) for i in range(n)]) for k, b in enumerate(blocks, 1)]
        return came, tuple(came)
    up, down = blocks
    came_up = hop(up, [(i, (i + 1) % n) for i in range(n)])
    first = hop(down, [(1, 0), (2, 1), (0, 3)])
    came_up, first = lax.optimization_barrier((came_up, first))
    second = hop(first, [(3, 2)])
    return [came_up, jnp.where(x == 2, second, first)], (came_up, first)


def gather_weight(out_weight, x, core, line):
    left, right = jnp.split(out_weight, 2, axis=1)
    got = swap(jnp.where(core == 0, right, left))
    kept = jnp.where(core == 0, left, right)
    rows = jnp.concatenate([jnp.where(core == 0, kept, got), jnp.where(core == 0, got, kept)])
    back = [hop(rows, [(i, (i + k) % line) for i in range(line)]) for k in range(line - 1, 0, -1)]
    ring = jnp.stack([*back, rows] * 2)
    ordered = lax.dynamic_slice_in_dim(ring, line - 1 - x, line, 0)
    return lax.all_gather(ordered.reshape(-1, rows.shape[1]), "dp", axis=0, tiled=True)


def run(n, line, place, out_weight, *tensors):
    heads = tensors[0].shape[1] // HEAD_DIM // n
    rounds = heads // CORES
    x, c = place[2], place[3]
    phases, results = [], []

    def send(blocks):
        if len(phases) >= 2:
            blocks = list(after(tuple(blocks), phases[-2]))
        came, done = turn(blocks, line, x)
        phases.append(done)
        return came

    for r in range(rounds):
        if r == 0 or (n < line and r == rounds - 1):
            kept, *sent = keep(place, tensors, n, heads, r)
            pieces = [("own", [kept, *send(sent)])]
            if r == 0:
                later = after(place, kept)
                got_first = swap(give(later, tensors, n, heads, (0,)))
                later = after(place, got_first)
                got_rest = swap(give(later, tensors, n, heads, tuple(range(1, rounds))))
                got = got_first[0]
            else:
                got = got_rest[r - 1]
            kept, *sent = [got[k] for k in range(n)]
            pieces.append(("other", [kept, *send(sent)]))
        else:
            kept, *sent = merge(place, tensors, got_rest, n, heads, r, r - 1)
            pieces = [("both", [kept, *send(sent)])]
        if r == 0:
            w_own = gather_weight(after(out_weight, got_first), x, c, line)
        results.append(attend(place, pieces))
    w_other = swap(after(w_own, phases[-2]))
    mine, others = [], []
    for group in (results[:-1], results[-1:]):
        kept, *sent = [jnp.stack([r[k] for r in group]) for k in range(n)]
        whole = [kept, *send(sent)]
        rows = tensors[0].shape[0]
        theirs = [lax.dynamic_slice_in_dim(t, (1 - c) * rows, rows, 2) for t in whole]
        mine.append(whole)
        others.append(swap(jnp.stack(theirs, axis=1)))
    return tuple(project(place, mine, others, w_own, w_other, n, heads))


def shards(q, k, v, dq, dk, dv, out_weight, frame_counts, token_offsets, video_group):
    members, groups = lax.axis_size("ulysses"), lax.axis_size("dp")
    line = members // CORES
    per_chip = CORES * q.shape[0] // FRAME
    u = lax.axis_index("ulysses")
    mine = video_group == lax.axis_index("dp")
    place = jnp.stack(
        [
            jnp.sum(jnp.where(mine & (token_offsets == 0), frame_counts, 0)),
            jnp.sum(jnp.where(mine & (token_offsets > 0), frame_counts, 0)),
            u // CORES,
            u % CORES,
        ]
    ).astype(jnp.int32)
    in_group = video_group[None, :] == jnp.arange(groups, dtype=video_group.dtype)[:, None]
    most = jnp.max(jnp.sum(jnp.where(in_group, frame_counts[None, :], 0), axis=1))
    return lax.cond(
        most <= (line - 1) * per_chip,
        functools.partial(run, line - 1, line),
        functools.partial(run, line, line),
        place,
        out_weight,
        q,
        k,
        v,
        dq,
        dk,
        dv,
    )


def solution(mesh):
    split = P(("dp", "ulysses"), None)
    return jax.shard_map(
        shards,
        mesh=mesh,
        in_specs=(split,) * 7 + (P(),) * 3,
        out_specs=(split, split),
        check_vma=False,
    )
```

```python
import functools
import math

import jax
import jax.numpy as jnp
from jax import lax
from jax.experimental import pallas as pl
from jax.experimental.pallas import tpu as pltpu
from jax.sharding import PartitionSpec as P

HEAD_DIM = 128
FRAME = 128
FRAMES_MOST = 8
CORES = 2
LOG2E = 1.4426950408889634
BF16 = jnp.bfloat16
ANY = pl.BlockSpec(memory_space=pl.ANY)
SMEM = pl.BlockSpec(memory_space=pltpu.SMEM)
VMEM = pl.BlockSpec(memory_space=pltpu.VMEM)


def run_copies(pairs, sems):
    copies = [pltpu.make_async_copy(a, b, sems.at[i]) for i, (a, b) in enumerate(pairs)]
    for copy in copies:
        copy.start()
    for copy in copies:
        copy.wait()


def pack_kernel(r, rounds, *refs):
    tensors, out, sems = refs[:6], refs[6], refs[7]
    pairs = []
    for u in range(out.shape[0]):
        at = slice((u * rounds + r) * HEAD_DIM, (u * rounds + r + 1) * HEAD_DIM)
        pairs += [(tensors[t].at[:, at], out.at[u, t]) for t in range(6)]
    run_copies(pairs, sems)


def pack(tensors, r, rounds, members):
    rows = tensors[0].shape[0]
    return pl.pallas_call(
        functools.partial(pack_kernel, r, rounds),
        in_specs=[ANY] * 6,
        out_specs=VMEM,
        out_shape=jax.ShapeDtypeStruct((members, 6, rows, HEAD_DIM), BF16),
        scratch_shapes=[pltpu.SemaphoreType.DMA((6 * members,))],
        name="pack",
    )(*tensors)


def nt_dot(a, b):
    return lax.dot_general(a, b, (((1,), (1,)), ((), ())), preferred_element_type=jnp.float32)


def attend_kernel(info, x, out, qq, kk, vv, sems):
    members, _, rows, _ = x.shape
    per = rows // FRAME
    first_count, second_count = info[0], info[1]
    used = first_count + second_count
    factor = LOG2E / math.sqrt(HEAD_DIM)
    scale = 1.0 / math.sqrt(HEAD_DIM)

    pairs = []
    for u in range(members):
        at = slice(u * rows, (u + 1) * rows)
        for t, (to, half) in enumerate(((qq, 1), (kk, 0), (vv, 0), (qq, 0), (kk, 1), (vv, 1))):
            pairs.append((x.at[u, t], to.at[at, half * HEAD_DIM : (half + 1) * HEAD_DIM]))
    run_copies(pairs, sems)

    def store(frame, which, value):
        at = pl.multiple_of(lax.rem(frame, per) * FRAME, FRAME)
        out[lax.div(frame, per), which, pl.ds(at, FRAME), :] = value

    def one_video(start, count):
        keys = pl.ds(pl.multiple_of(start * FRAME, FRAME), count * FRAME)

        def block(frame, frames):
            at = pl.ds(pl.multiple_of(frame * FRAME, FRAME), frames * FRAME)
            s = nt_dot(qq[at, HEAD_DIM:], kk[keys, :HEAD_DIM]) * factor
            t = nt_dot(qq[at, :], kk[keys, :]) * scale
            e = jnp.exp2(s - jnp.max(s, axis=1, keepdims=True))
            p = e * (1.0 / jnp.sum(e, axis=1, keepdims=True))
            mean = jnp.sum(p * t, axis=1, keepdims=True)
            low = p.astype(BF16)
            turned = (p * (t - mean)).astype(BF16)
            both = jnp.dot(low, vv[keys, :], preferred_element_type=jnp.float32)
            more = jnp.dot(turned, vv[keys, :HEAD_DIM], preferred_element_type=jnp.float32)
            primal = both[:, :HEAD_DIM].astype(BF16)
            tangent = (both[:, HEAD_DIM:] + more).astype(BF16)
            for i in range(frames):
                part = slice(i * FRAME, (i + 1) * FRAME)
                store(frame + i, 0, primal[part])
                store(frame + i, 1, tangent[part])

        def two_frames(i, carry):
            block(start + 2 * i, 2)
            return carry

        lax.fori_loop(0, count // 2, two_frames, 0)
        if count % 2:
            block(start + count - 1, 1)

    def video(i, carry):
        start = jnp.where(i == 0, 0, first_count)
        count = jnp.where(i == 0, first_count, second_count)
        for frames in range(1, FRAMES_MOST + 1):
            pl.when(count == frames)(functools.partial(one_video, start, frames))
        return carry

    lax.fori_loop(0, 2, video, 0)

    def blank(frame, carry):
        nothing = jnp.zeros((FRAME, HEAD_DIM), BF16)
        store(frame, 0, nothing)
        store(frame, 1, nothing)
        return carry

    lax.fori_loop(used, members * per, blank, 0)


def attend(info, x):
    members, _, rows, _ = x.shape
    return pl.pallas_call(
        attend_kernel,
        in_specs=[SMEM, ANY],
        out_specs=VMEM,
        out_shape=jax.ShapeDtypeStruct((members, 2, rows, HEAD_DIM), BF16),
        scratch_shapes=[pltpu.VMEM((members * rows, 2 * HEAD_DIM), BF16)] * 3
        + [pltpu.SemaphoreType.DMA((6 * members,))],
        compiler_params=pltpu.CompilerParams(vmem_limit_bytes=40 * 2**20),
        name="attend",
    )(info, x)


def project_kernel(moved, w, *refs):
    if len(refs) == 5:
        total, out, tangent, held, sems = refs
    else:
        out, held, sems = refs
        total = None
    members, size, _, rows, _ = moved.shape

    @pl.when(pl.program_id(0) == 0)
    def _():
        pairs = []
        for u in range(members):
            for i in range(size):
                at = slice((u * size + i) * HEAD_DIM, (u * size + i + 1) * HEAD_DIM)
                for which in range(2):
                    down = slice(which * rows, (which + 1) * rows)
                    pairs.append((moved.at[u, i, which], held.at[down, at]))
        run_copies(pairs, sems)

    depth = held.shape[1]
    product = jnp.dot(held[...], w[...].reshape(depth, -1), preferred_element_type=jnp.float32)
    if total is None:
        out[...] = product
    else:
        out[...] = (total[:rows] + product[:rows]).astype(BF16)
        tangent[...] = (total[rows:] + product[rows:]).astype(BF16)


def project(moved, weight, rounds, first, total=None):
    members, size, _, rows, _ = moved.shape
    width = weight.shape[1]
    tile = 512
    by_round = weight.reshape(members, rounds, HEAD_DIM, width)
    sum_spec = pl.BlockSpec((2 * rows, tile), lambda step: (0, step))
    half_spec = pl.BlockSpec((rows, tile), lambda step: (0, step))
    last = total is not None
    return pl.pallas_call(
        project_kernel,
        grid=(width // tile,),
        in_specs=[ANY]
        + [pl.BlockSpec((members, size, HEAD_DIM, tile), lambda step: (0, first // size, 0, step))]
        + [sum_spec] * last,
        out_specs=[half_spec, half_spec] if last else sum_spec,
        scratch_shapes=[
            pltpu.VMEM((2 * rows, members * size * HEAD_DIM), BF16),
            pltpu.SemaphoreType.DMA((2 * members * size,)),
        ],
        out_shape=[jax.ShapeDtypeStruct((rows, width), BF16)] * 2
        if last
        else jax.ShapeDtypeStruct((2 * rows, width), jnp.float32),
        compiler_params=pltpu.CompilerParams(vmem_limit_bytes=40 * 2**20),
        name="project",
    )(moved, by_round, *([total] if last else []))


def after(value, *done):
    return lax.optimization_barrier((value, done))[0]


def exchange(x):
    return lax.all_to_all(x, "ulysses", split_axis=0, concat_axis=0, tiled=True)


def hop(value, chips):
    pairs = [(a * CORES + c, b * CORES + c) for a, b in chips for c in range(CORES)]
    return lax.ppermute(value, "ulysses", pairs)


def swap(value):
    members = lax.axis_size("ulysses")
    return lax.ppermute(value, "ulysses", [(u, u ^ 1) for u in range(members)])


def gather_line(shard, ready):
    u = lax.axis_index("ulysses")
    x, core = u // CORES, u % CORES
    line = lax.axis_size("ulysses") // CORES
    back = [hop(shard, [(i, (i + k) % line) for i in range(line)]) for k in range(line - 1, 0, -1)]
    back = after(tuple(back), ready)
    ring = jnp.stack([*back, shard] * 2)
    mine = lax.dynamic_slice_in_dim(ring, line - 1 - x, line, 0)
    theirs = swap(mine)
    pair = [jnp.where(core == 0, mine, theirs), jnp.where(core == 0, theirs, mine)]
    return jnp.stack(pair, axis=1).reshape(-1, shard.shape[1])


def shards(q, k, v, dq, dk, dv, out_weight, frame_counts, token_offsets, video_group):
    members = lax.axis_size("ulysses")
    rounds = q.shape[1] // HEAD_DIM // members
    tensors = (q, k, v, dq, dk, dv)
    packed = [pack(tensors, 0, rounds, members)]
    near = gather_line(out_weight, packed[0])
    weight = lax.all_gather(near, "dp", axis=0, tiled=True)
    arrived = exchange(packed[0])
    mine = video_group == lax.axis_index("dp")
    info = jnp.stack(
        [
            jnp.sum(jnp.where(mine & (token_offsets == 0), frame_counts, 0)),
            jnp.sum(jnp.where(mine & (token_offsets > 0), frame_counts, 0)),
        ]
    ).astype(jnp.int32)
    results = []
    for r in range(1, rounds):
        sent = pack(tensors, r, rounds, members)
        sent, arrived = lax.optimization_barrier((sent, arrived))
        came = exchange(sent)
        results.append(attend(info, arrived))
        arrived = came
    sent = jnp.stack(results, axis=1)
    sent, arrived = lax.optimization_barrier((sent, arrived))
    came = exchange(sent)
    sent = attend(info, arrived)[:, None]
    sent, came, weight = lax.optimization_barrier((sent, came, weight))
    last = exchange(sent)
    total = project(came, weight, rounds, 0)
    return tuple(project(last, weight, rounds, rounds - 1, total))


def solution(mesh):
    split = P(("dp", "ulysses"), None)
    return jax.shard_map(
        shards,
        mesh=mesh,
        in_specs=(split,) * 7 + (P(),) * 3,
        out_specs=(split, split),
        check_vma=False,
    )
```

```python
import functools
import math

import jax
import jax.numpy as jnp
from jax import lax
from jax.experimental import pallas as pl
from jax.experimental.pallas import tpu as pltpu
from jax.sharding import PartitionSpec as P

HEAD_DIM = 128
FRAME = 128
FRAMES_MOST = 8
CORES = 2
LOG2E = 1.4426950408889634
BF16 = jnp.bfloat16
ANY = pl.BlockSpec(memory_space=pl.ANY)
SMEM = pl.BlockSpec(memory_space=pltpu.SMEM)
VMEM = pl.BlockSpec(memory_space=pltpu.VMEM)


def run_copies(pairs, sems):
    copies = [pltpu.make_async_copy(a, b, sems.at[i]) for i, (a, b) in enumerate(pairs)]
    for copy in copies:
        copy.start()
    for copy in copies:
        copy.wait()


def member(block, members, back=False):
    u = lax.axis_index("ulysses")
    x, c = lax.div(u, CORES), lax.rem(u, CORES)
    line = members // CORES
    k, f = block // CORES, block % CORES
    return lax.rem(x + (line - k if back else k), line) * CORES + (1 - c if f else c)


def pack_kernel(first, rounds, members, blocks, *refs):
    tensors, outs, (held, sems, out_sems) = refs[:6], refs[6:-3], refs[-3:]
    size = outs[0].shape[0]
    loads, stores = [], []
    for j, b in enumerate(blocks):
        for i in range(size):
            head = member(b, members) * rounds + first + i
            at = pl.ds(pl.multiple_of(head * HEAD_DIM, HEAD_DIM), HEAD_DIM)
            for t in range(6):
                source, to = tensors[t].at[:, at], held.at[j, i, t]
                loads.append(pltpu.make_async_copy(source, to, sems.at[j, i, t]))
        stores.append(pltpu.make_async_copy(held.at[j], outs[j], out_sems.at[j]))
    for load in loads:
        load.start()
    for j, store in enumerate(stores):
        for load in loads[j * size * 6 : (j + 1) * size * 6]:
            load.wait()
        store.start()
    for store in stores:
        store.wait()


def pack(tensors, first, size, rounds, members, blocks):
    rows = tensors[0].shape[0]
    count = len(blocks)
    return pl.pallas_call(
        functools.partial(pack_kernel, first, rounds, members, blocks),
        in_specs=[ANY] * 6,
        out_specs=[ANY] * count,
        out_shape=[jax.ShapeDtypeStruct((size, 6, rows, HEAD_DIM), BF16)] * count,
        scratch_shapes=[
            pltpu.VMEM((count, size, 6, rows, HEAD_DIM), BF16),
            pltpu.SemaphoreType.DMA((count, size, 6)),
            pltpu.SemaphoreType.DMA((count,)),
        ],
        name="pack",
    )(*tensors)


def nt_dot(a, b):
    return lax.dot_general(a, b, (((1,), (1,)), ((), ())), preferred_element_type=jnp.float32)


def attend_kernel(members, info, *refs):
    moved, (out, qq, kk, vv, sems) = refs[:members], refs[members:]
    size, _, rows, _ = moved[0].shape
    per = rows // FRAME
    first_count, second_count = info[0], info[1]
    used = first_count + second_count
    factor = LOG2E / math.sqrt(HEAD_DIM)
    scale = 1.0 / math.sqrt(HEAD_DIM)

    def store(head, frame, which, value):
        at = pl.multiple_of(lax.rem(frame, per) * FRAME, FRAME)
        out[lax.div(frame, per), head, which, pl.ds(at, FRAME), :] = value

    def one_video(head, start, count):
        keys = pl.ds(pl.multiple_of(start * FRAME, FRAME), count * FRAME)

        def block(frame, frames):
            at = pl.ds(pl.multiple_of(frame * FRAME, FRAME), frames * FRAME)
            s = nt_dot(qq[at, HEAD_DIM:], kk[keys, :HEAD_DIM]) * factor
            t = nt_dot(qq[at, :], kk[keys, :]) * scale
            e = jnp.exp2(s - jnp.max(s, axis=1, keepdims=True))
            p = e * (1.0 / jnp.sum(e, axis=1, keepdims=True))
            mean = jnp.sum(p * t, axis=1, keepdims=True)
            low = p.astype(BF16)
            turned = (p * (t - mean)).astype(BF16)
            both = jnp.dot(low, vv[keys, :], preferred_element_type=jnp.float32)
            more = jnp.dot(turned, vv[keys, :HEAD_DIM], preferred_element_type=jnp.float32)
            primal = both[:, :HEAD_DIM].astype(BF16)
            tangent = (both[:, HEAD_DIM:] + more).astype(BF16)
            for i in range(frames):
                part = slice(i * FRAME, (i + 1) * FRAME)
                store(head, frame + i, 0, primal[part])
                store(head, frame + i, 1, tangent[part])

        def two_frames(i, carry):
            block(start + 2 * i, 2)
            return carry

        lax.fori_loop(0, count // 2, two_frames, 0)
        if count % 2:
            block(start + count - 1, 1)

    def one_head(head, carry):
        pairs = []
        for b in range(members):
            at = pl.ds(pl.multiple_of(member(b, members, True) * rows, rows), rows)
            for t, (to, half) in enumerate(((qq, 1), (kk, 0), (vv, 0), (qq, 0), (kk, 1), (vv, 1))):
                part = slice(half * HEAD_DIM, (half + 1) * HEAD_DIM)
                pairs.append((moved[b].at[head, t], to.at[at, part]))
        run_copies(pairs, sems)

        def video(i, carry):
            start = jnp.where(i == 0, 0, first_count)
            count = jnp.where(i == 0, first_count, second_count)
            for frames in range(1, FRAMES_MOST + 1):
                pl.when(count == frames)(functools.partial(one_video, head, start, frames))
            return carry

        def blank(frame, carry):
            nothing = jnp.zeros((FRAME, HEAD_DIM), BF16)
            store(head, frame, 0, nothing)
            store(head, frame, 1, nothing)
            return carry

        lax.fori_loop(0, 2, video, 0)
        lax.fori_loop(used, members * per, blank, 0)
        return carry

    lax.fori_loop(0, size, one_head, 0)


def attend(info, moved):
    members = len(moved)
    size, _, rows, _ = moved[0].shape
    return pl.pallas_call(
        functools.partial(attend_kernel, members),
        in_specs=[SMEM] + [ANY] * members,
        out_specs=VMEM,
        out_shape=jax.ShapeDtypeStruct((members, size, 2, rows, HEAD_DIM), BF16),
        scratch_shapes=[pltpu.VMEM((members * rows, 2 * HEAD_DIM), BF16)] * 3
        + [pltpu.SemaphoreType.DMA((6 * members,))],
        compiler_params=pltpu.CompilerParams(vmem_limit_bytes=40 * 2**20),
        name="attend",
    )(info, *moved)


def project_kernel(moved, w, *refs):
    if len(refs) == 5:
        total, out, tangent, held, sems = refs
    else:
        out, held, sems = refs
        total = None
    members, size, _, rows, _ = moved.shape

    @pl.when(pl.program_id(0) == 0)
    def _():
        pairs = []
        for u in range(members):
            for i in range(size):
                at = slice((u * size + i) * HEAD_DIM, (u * size + i + 1) * HEAD_DIM)
                for which in range(2):
                    down = slice(which * rows, (which + 1) * rows)
                    pairs.append((moved.at[u, i, which], held.at[down, at]))
        run_copies(pairs, sems)

    depth = held.shape[1]
    product = jnp.dot(held[...], w[...].reshape(depth, -1), preferred_element_type=jnp.float32)
    if total is None:
        out[...] = product
    else:
        out[...] = (total[:rows] + product[:rows]).astype(BF16)
        tangent[...] = (total[rows:] + product[rows:]).astype(BF16)


def project(moved, weight, rounds, first, total=None):
    members, size, _, rows, _ = moved.shape
    width = weight.shape[1]
    tile = 512
    by_round = weight.reshape(members, rounds, HEAD_DIM, width)
    sum_spec = pl.BlockSpec((2 * rows, tile), lambda step: (0, step))
    half_spec = pl.BlockSpec((rows, tile), lambda step: (0, step))
    last = total is not None
    return pl.pallas_call(
        project_kernel,
        grid=(width // tile,),
        in_specs=[ANY]
        + [pl.BlockSpec((members, size, HEAD_DIM, tile), lambda step: (0, first // size, 0, step))]
        + [sum_spec] * last,
        out_specs=[half_spec, half_spec] if last else sum_spec,
        scratch_shapes=[
            pltpu.VMEM((2 * rows, members * size * HEAD_DIM), BF16),
            pltpu.SemaphoreType.DMA((2 * members * size,)),
        ],
        out_shape=[jax.ShapeDtypeStruct((rows, width), BF16)] * 2
        if last
        else jax.ShapeDtypeStruct((2 * rows, width), jnp.float32),
        compiler_params=pltpu.CompilerParams(vmem_limit_bytes=56 * 2**20),
        name="project",
    )(moved, by_round, *([total] if last else []))


def after(value, *done):
    return lax.optimization_barrier((value, done))[0]


def hop(value, k, f=0):
    members = lax.axis_size("ulysses")
    pairs = [(u, (u + k * CORES) % members ^ f) for u in range(members)]
    return lax.ppermute(value, "ulysses", pairs)


def gather_line(shard, ready):
    u = lax.axis_index("ulysses")
    x, core = u // CORES, u % CORES
    line = lax.axis_size("ulysses") // CORES
    back = [hop(shard, k) for k in range(line - 1, 0, -1)]
    back = after(tuple(back), ready)
    ring = jnp.stack([*back, shard] * 2)
    mine = lax.dynamic_slice_in_dim(ring, line - 1 - x, line, 0)
    theirs = hop(mine, 0, 1)
    pair = [jnp.where(core == 0, mine, theirs), jnp.where(core == 0, theirs, mine)]
    return jnp.stack(pair, axis=1).reshape(-1, shard.shape[1])


def exchange(x):
    return lax.all_to_all(x, "ulysses", split_axis=0, concat_axis=0, tiled=True)


def send(blocks):
    return {b: hop(block, b // CORES, b % CORES) if b else block for b, block in blocks.items()}


def shards(q, k, v, dq, dk, dv, out_weight, frame_counts, token_offsets, video_group):
    members = lax.axis_size("ulysses")
    rounds = q.shape[1] // HEAD_DIM // members
    tensors = (q, k, v, dq, dk, dv)
    same = tuple(range(CORES, members, CORES))
    other = tuple(range(CORES + 1, members, CORES)) + (1, 0)

    def packed(first, size, blocks):
        return dict(zip(blocks, pack(tensors, first, size, rounds, members, blocks)))

    def in_order(arrived):
        return [arrived[b] for b in range(members)]

    early = packed(0, rounds - 1, same) | packed(0, rounds - 1, other)
    near = gather_line(out_weight, early)
    weight = lax.all_gather(near, "dp", axis=0, tiled=True)
    arrived = in_order(send(early))
    mine = video_group == lax.axis_index("dp")
    info = jnp.stack(
        [
            jnp.sum(jnp.where(mine & (token_offsets == 0), frame_counts, 0)),
            jnp.sum(jnp.where(mine & (token_offsets > 0), frame_counts, 0)),
        ]
    ).astype(jnp.int32)
    late = packed(rounds - 1, 1, same + other)
    late, arrived = lax.optimization_barrier((late, arrived))
    late, result = in_order(send(late)), attend(info, arrived)
    result, late = lax.optimization_barrier((result, late))
    moved, result = exchange(result), attend(info, late)
    result, moved, weight = lax.optimization_barrier((result, moved, weight))
    last, total = exchange(result), project(moved, weight, rounds, 0)
    return tuple(project(last, weight, rounds, rounds - 1, total))


def solution(mesh):
    split = P(("dp", "ulysses"), None)
    return jax.shard_map(
        shards,
        mesh=mesh,
        in_specs=(split,) * 7 + (P(),) * 3,
        out_specs=(split, split),
        check_vma=False,
    )
```

```python
import functools
import math

import jax
import jax.numpy as jnp
from jax import lax
from jax.experimental import pallas as pl
from jax.experimental.pallas import tpu as pltpu
from jax.sharding import PartitionSpec as P

HEAD_DIM = 128
FRAME = 128
FRAMES_MOST = 8
CORES = 2
LOG2E = 1.4426950408889634
BF16 = jnp.bfloat16
ANY = pl.BlockSpec(memory_space=pl.ANY)
SMEM = pl.BlockSpec(memory_space=pltpu.SMEM)
VMEM = pl.BlockSpec(memory_space=pltpu.VMEM)


def run_copies(pairs, sems):
    copies = [pltpu.make_async_copy(a, b, sems.at[i]) for i, (a, b) in enumerate(pairs)]
    for copy in copies:
        copy.start()
    for copy in copies:
        copy.wait()


def member(block, members, back=False):
    u = lax.axis_index("ulysses")
    x, c = lax.div(u, CORES), lax.rem(u, CORES)
    line = members // CORES
    k, f = block // CORES, block % CORES
    return lax.rem(x + (line - k if back else k), line) * CORES + (1 - c if f else c)


def pack_kernel(first, rounds, members, blocks, *refs):
    tensors, outs, (held, sems, out_sems) = refs[:6], refs[6:-3], refs[-3:]
    size = outs[0].shape[0]
    loads, stores = [], []
    for j, b in enumerate(blocks):
        for i in range(size):
            head = member(b, members) * rounds + first + i
            at = pl.ds(pl.multiple_of(head * HEAD_DIM, HEAD_DIM), HEAD_DIM)
            for t in range(6):
                source, to = tensors[t].at[:, at], held.at[j, i, t]
                loads.append(pltpu.make_async_copy(source, to, sems.at[j, i, t]))
        stores.append(pltpu.make_async_copy(held.at[j], outs[j], out_sems.at[j]))
    for load in loads:
        load.start()
    for j, store in enumerate(stores):
        for load in loads[j * size * 6 : (j + 1) * size * 6]:
            load.wait()
        store.start()
    for store in stores:
        store.wait()


def pack(tensors, first, size, rounds, members, blocks):
    rows = tensors[0].shape[0]
    count = len(blocks)
    return pl.pallas_call(
        functools.partial(pack_kernel, first, rounds, members, blocks),
        in_specs=[ANY] * 6,
        out_specs=[ANY] * count,
        out_shape=[jax.ShapeDtypeStruct((size, 6, rows, HEAD_DIM), BF16)] * count,
        scratch_shapes=[
            pltpu.VMEM((count, size, 6, rows, HEAD_DIM), BF16),
            pltpu.SemaphoreType.DMA((count, size, 6)),
            pltpu.SemaphoreType.DMA((count,)),
        ],
        name="pack",
    )(*tensors)


def nt_dot(a, b):
    return lax.dot_general(a, b, (((1,), (1,)), ((), ())), preferred_element_type=jnp.float32)


def attend_kernel(members, apart, info, *refs):
    moved, outs, (qq, kk, vv, sems) = refs[:members], refs[members:-4], refs[-4:]
    if apart:
        *outs, out = outs
    else:
        (out,) = outs
    size, _, rows, _ = moved[0].shape
    per = rows // FRAME
    first_count, second_count = info[0], info[1]
    used = first_count + second_count
    factor = LOG2E / math.sqrt(HEAD_DIM)
    scale = 1.0 / math.sqrt(HEAD_DIM)

    def store(head, frame, which, value):
        at = pl.multiple_of(lax.rem(frame, per) * FRAME, FRAME)
        out[lax.div(frame, per), head, which, pl.ds(at, FRAME), :] = value

    def one_video(head, start, count):
        keys = pl.ds(pl.multiple_of(start * FRAME, FRAME), count * FRAME)

        def block(frame, frames):
            at = pl.ds(pl.multiple_of(frame * FRAME, FRAME), frames * FRAME)
            s = nt_dot(qq[at, HEAD_DIM:], kk[keys, :HEAD_DIM]) * factor
            t = nt_dot(qq[at, :], kk[keys, :]) * scale
            e = jnp.exp2(s - jnp.max(s, axis=1, keepdims=True))
            p = e * (1.0 / jnp.sum(e, axis=1, keepdims=True))
            mean = jnp.sum(p * t, axis=1, keepdims=True)
            low = p.astype(BF16)
            turned = (p * (t - mean)).astype(BF16)
            both = jnp.dot(low, vv[keys, :], preferred_element_type=jnp.float32)
            more = jnp.dot(turned, vv[keys, :HEAD_DIM], preferred_element_type=jnp.float32)
            primal = both[:, :HEAD_DIM].astype(BF16)
            tangent = (both[:, HEAD_DIM:] + more).astype(BF16)
            for i in range(frames):
                part = slice(i * FRAME, (i + 1) * FRAME)
                store(head, frame + i, 0, primal[part])
                store(head, frame + i, 1, tangent[part])

        def two_frames(i, carry):
            block(start + 2 * i, 2)
            return carry

        lax.fori_loop(0, count // 2, two_frames, 0)
        if count % 2:
            block(start + count - 1, 1)

    def one_head(head, carry):
        pairs = []
        for b in range(members):
            at = pl.ds(pl.multiple_of(member(b, members, True) * rows, rows), rows)
            for t, (to, half) in enumerate(((qq, 1), (kk, 0), (vv, 0), (qq, 0), (kk, 1), (vv, 1))):
                part = slice(half * HEAD_DIM, (half + 1) * HEAD_DIM)
                pairs.append((moved[b].at[head, t], to.at[at, part]))
        run_copies(pairs, sems)

        def video(i, carry):
            start = jnp.where(i == 0, 0, first_count)
            count = jnp.where(i == 0, first_count, second_count)
            for frames in range(1, FRAMES_MOST + 1):
                pl.when(count == frames)(functools.partial(one_video, head, start, frames))
            return carry

        def blank(frame, carry):
            nothing = jnp.zeros((FRAME, HEAD_DIM), BF16)
            store(head, frame, 0, nothing)
            store(head, frame, 1, nothing)
            return carry

        lax.fori_loop(0, 2, video, 0)
        lax.fori_loop(used, members * per, blank, 0)
        return carry

    lax.fori_loop(0, size, one_head, 0)
    if apart:
        for b in range(members):
            outs[b][...] = out[member(b, members)]


def attend(info, moved, apart=False):
    members = len(moved)
    size, _, rows, _ = moved[0].shape
    whole = (members, size, 2, rows, HEAD_DIM)
    block = jax.ShapeDtypeStruct(whole[1:], BF16)
    return pl.pallas_call(
        functools.partial(attend_kernel, members, apart),
        in_specs=[SMEM] + [ANY] * members,
        out_specs=[VMEM] * members if apart else VMEM,
        out_shape=[block] * members if apart else jax.ShapeDtypeStruct(whole, BF16),
        scratch_shapes=[pltpu.VMEM(whole, BF16)] * apart
        + [pltpu.VMEM((members * rows, 2 * HEAD_DIM), BF16)] * 3
        + [pltpu.SemaphoreType.DMA((6 * members,))],
        compiler_params=pltpu.CompilerParams(vmem_limit_bytes=40 * 2**20),
        name="attend",
    )(info, *moved)


def project_kernel(members, moved, *refs):
    last, (w, out, tangent, held, sems) = refs[:members], refs[members:]
    _, size, _, rows, _ = moved.shape
    rounds = size + last[0].shape[0]

    @pl.when(pl.program_id(0) == 0)
    def _():
        pairs = []
        for b in range(members):
            u = member(b, members, True)
            for r in range(rounds):
                for which in range(2):
                    source = moved.at[b, r, which] if r < size else last[b].at[r - size, which]
                    head = (b if r < size else u) * rounds + r
                    at = pl.ds(pl.multiple_of(head * HEAD_DIM, HEAD_DIM), HEAD_DIM)
                    pairs.append((source, held.at[which * rows : (which + 1) * rows, at]))
        run_copies(pairs, sems)

    product = jnp.dot(held[...], w[...], preferred_element_type=jnp.float32)
    out[...] = product[:rows].astype(BF16)
    tangent[...] = product[rows:].astype(BF16)


def project(moved, last, weight):
    members, size, _, rows, _ = moved.shape
    depth, width = weight.shape
    tile = 768
    given = pl.BlockSpec((rows, tile), lambda step: (0, step))
    return pl.pallas_call(
        functools.partial(project_kernel, members),
        grid=(width // tile,),
        in_specs=[ANY] * (1 + members) + [pl.BlockSpec((depth, tile), lambda step: (0, step))],
        out_specs=[given, given],
        out_shape=[jax.ShapeDtypeStruct((rows, width), BF16)] * 2,
        scratch_shapes=[
            pltpu.VMEM((2 * rows, depth), BF16),
            pltpu.SemaphoreType.DMA((2 * depth // HEAD_DIM,)),
        ],
        compiler_params=pltpu.CompilerParams(vmem_limit_bytes=40 * 2**20),
        name="project",
    )(moved, *last, weight)


def after(value, *done):
    return lax.optimization_barrier((value, done))[0]


def hop(value, k, f=0):
    members = lax.axis_size("ulysses")
    pairs = [(u, (u + k * CORES) % members ^ f) for u in range(members)]
    return lax.ppermute(value, "ulysses", pairs)


def gather_line(shard, ready):
    u = lax.axis_index("ulysses")
    x, core = u // CORES, u % CORES
    line = lax.axis_size("ulysses") // CORES
    back = [hop(shard, k) for k in range(line - 1, 0, -1)]
    back = after(tuple(back), ready)
    ring = jnp.stack([*back, shard] * 2)
    mine = lax.dynamic_slice_in_dim(ring, line - 1 - x, line, 0)
    theirs = hop(mine, 0, 1)
    pair = [jnp.where(core == 0, mine, theirs), jnp.where(core == 0, theirs, mine)]
    return jnp.stack(pair, axis=1).reshape(-1, shard.shape[1])


def exchange(x):
    return lax.all_to_all(x, "ulysses", split_axis=0, concat_axis=0, tiled=True)


def send(blocks):
    return {b: hop(block, b // CORES, b % CORES) if b else block for b, block in blocks.items()}


def shards(q, k, v, dq, dk, dv, out_weight, frame_counts, token_offsets, video_group):
    members = lax.axis_size("ulysses")
    rounds = q.shape[1] // HEAD_DIM // members
    tensors = (q, k, v, dq, dk, dv)
    same = tuple(range(CORES, members, CORES))
    other = tuple(range(CORES + 1, members, CORES)) + (1, 0)

    def packed(first, size, blocks):
        return dict(zip(blocks, pack(tensors, first, size, rounds, members, blocks)))

    def in_order(arrived):
        return [arrived[b] for b in range(members)]

    early = packed(0, rounds - 1, same) | packed(0, rounds - 1, other)
    near = gather_line(out_weight, early)
    weight = lax.all_gather(near, "dp", axis=0, tiled=True)
    arrived = in_order(send(early))
    mine = video_group == lax.axis_index("dp")
    info = jnp.stack(
        [
            jnp.sum(jnp.where(mine & (token_offsets == 0), frame_counts, 0)),
            jnp.sum(jnp.where(mine & (token_offsets > 0), frame_counts, 0)),
        ]
    ).astype(jnp.int32)
    late = packed(rounds - 1, 1, same + other)
    ready = [arrived[b] for b in same]
    late, ready = lax.optimization_barrier((late, ready))
    arrived = [ready[same.index(b)] if b in same else arrived[b] for b in range(members)]
    late, result = in_order(send(late)), attend(info, arrived)
    result, late = lax.optimization_barrier((result, late))
    moved = exchange(result)
    last = send(dict(enumerate(attend(info, late, True))))
    return tuple(project(moved, in_order(last), weight))


def solution(mesh):
    split = P(("dp", "ulysses"), None)
    return jax.shard_map(
        shards,
        mesh=mesh,
        in_specs=(split,) * 7 + (P(),) * 3,
        out_specs=(split, split),
        check_vma=False,
    )
```

```python
import functools
import math

import jax
import jax.numpy as jnp
from jax import lax
from jax.experimental import pallas as pl
from jax.experimental.pallas import tpu as pltpu
from jax.sharding import PartitionSpec as P

HEAD_DIM = 128
FRAME = 128
FRAMES_MOST = 8
CORES = 2
LOG2E = 1.4426950408889634
BF16 = jnp.bfloat16
ANY = pl.BlockSpec(memory_space=pl.ANY)
SMEM = pl.BlockSpec(memory_space=pltpu.SMEM)
VMEM = pl.BlockSpec(memory_space=pltpu.VMEM)


def run_copies(pairs, sems):
    copies = [pltpu.make_async_copy(a, b, sems.at[i]) for i, (a, b) in enumerate(pairs)]
    for copy in copies:
        copy.start()
    for copy in copies:
        copy.wait()


def member(block, members, back=False):
    u = lax.axis_index("ulysses")
    x, c = lax.div(u, CORES), lax.rem(u, CORES)
    line = members // CORES
    k, f = block // CORES, block % CORES
    return lax.rem(x + (line - k if back else k), line) * CORES + (1 - c if f else c)


def pack_kernel(first, rounds, members, blocks, *refs):
    tensors, outs, (held, sems, out_sems) = refs[:6], refs[6:-3], refs[-3:]
    size = outs[0].shape[0]
    loads, stores = [], []
    for j, b in enumerate(blocks):
        for i in range(size):
            head = member(b, members) * rounds + first + i
            at = pl.ds(pl.multiple_of(head * HEAD_DIM, HEAD_DIM), HEAD_DIM)
            for t in range(6):
                source, to = tensors[t].at[:, at], held.at[j, i, t]
                loads.append(pltpu.make_async_copy(source, to, sems.at[j, i, t]))
        stores.append(pltpu.make_async_copy(held.at[j], outs[j], out_sems.at[j]))
    for load in loads:
        load.start()
    for j, store in enumerate(stores):
        for load in loads[j * size * 6 : (j + 1) * size * 6]:
            load.wait()
        store.start()
    for store in stores:
        store.wait()


def pack(tensors, first, size, rounds, members, blocks):
    rows = tensors[0].shape[0]
    count = len(blocks)
    return pl.pallas_call(
        functools.partial(pack_kernel, first, rounds, members, blocks),
        in_specs=[ANY] * 6,
        out_specs=[ANY] * count,
        out_shape=[jax.ShapeDtypeStruct((size, 6, rows, HEAD_DIM), BF16)] * count,
        scratch_shapes=[
            pltpu.VMEM((count, size, 6, rows, HEAD_DIM), BF16),
            pltpu.SemaphoreType.DMA((count, size, 6)),
            pltpu.SemaphoreType.DMA((count,)),
        ],
        name="pack",
    )(*tensors)


def nt_dot(a, b):
    return lax.dot_general(a, b, (((1,), (1,)), ((), ())), preferred_element_type=jnp.float32)


def attend_kernel(members, apart, info, *refs):
    moved, outs, (qq, kk, vv, sems) = refs[:members], refs[members:-4], refs[-4:]
    if apart:
        *outs, out = outs
    else:
        (out,) = outs
    size, _, rows, _ = moved[0].shape
    per = rows // FRAME
    first_count, second_count = info[0], info[1]
    used = first_count + second_count
    factor = LOG2E / math.sqrt(HEAD_DIM)
    scale = 1.0 / math.sqrt(HEAD_DIM)

    def store(head, frame, which, value):
        at = pl.multiple_of(lax.rem(frame, per) * FRAME, FRAME)
        out[lax.div(frame, per), head, which, pl.ds(at, FRAME), :] = value

    def one_video(head, start, count):
        keys = pl.ds(pl.multiple_of(start * FRAME, FRAME), count * FRAME)

        def block(frame, frames):
            at = pl.ds(pl.multiple_of(frame * FRAME, FRAME), frames * FRAME)
            s = nt_dot(qq[at, HEAD_DIM:], kk[keys, :HEAD_DIM]) * factor
            t = nt_dot(qq[at, :], kk[keys, :]) * scale
            e = jnp.exp2(s - jnp.max(s, axis=1, keepdims=True))
            p = e * (1.0 / jnp.sum(e, axis=1, keepdims=True))
            mean = jnp.sum(p * t, axis=1, keepdims=True)
            low = p.astype(BF16)
            turned = (p * (t - mean)).astype(BF16)
            both = jnp.dot(low, vv[keys, :], preferred_element_type=jnp.float32)
            more = jnp.dot(turned, vv[keys, :HEAD_DIM], preferred_element_type=jnp.float32)
            primal = both[:, :HEAD_DIM].astype(BF16)
            tangent = (both[:, HEAD_DIM:] + more).astype(BF16)
            for i in range(frames):
                part = slice(i * FRAME, (i + 1) * FRAME)
                store(head, frame + i, 0, primal[part])
                store(head, frame + i, 1, tangent[part])

        def four_frames(i, carry):
            block(start + 4 * i, 4)
            return carry

        lax.fori_loop(0, count // 4, four_frames, 0)
        if count % 4 >= 2:
            block(start + count - count % 4, 2)
        if count % 2:
            block(start + count - 1, 1)

    def one_head(head, carry):
        pairs = []
        for b in range(members):
            at = pl.ds(pl.multiple_of(member(b, members, True) * rows, rows), rows)
            for t, (to, half) in enumerate(((qq, 1), (kk, 0), (vv, 0), (qq, 0), (kk, 1), (vv, 1))):
                part = slice(half * HEAD_DIM, (half + 1) * HEAD_DIM)
                pairs.append((moved[b].at[head, t], to.at[at, part]))
        run_copies(pairs, sems)

        def video(i, carry):
            start = jnp.where(i == 0, 0, first_count)
            count = jnp.where(i == 0, first_count, second_count)
            for frames in range(1, FRAMES_MOST + 1):
                pl.when(count == frames)(functools.partial(one_video, head, start, frames))
            return carry

        def blank(frame, carry):
            nothing = jnp.zeros((FRAME, HEAD_DIM), BF16)
            store(head, frame, 0, nothing)
            store(head, frame, 1, nothing)
            return carry

        lax.fori_loop(0, 2, video, 0)
        lax.fori_loop(used, members * per, blank, 0)
        return carry

    lax.fori_loop(0, size, one_head, 0)
    if apart:
        for b in range(members):
            outs[b][...] = out[member(b, members)]


def attend(info, moved, apart=False):
    members = len(moved)
    size, _, rows, _ = moved[0].shape
    whole = (members, size, 2, rows, HEAD_DIM)
    block = jax.ShapeDtypeStruct(whole[1:], BF16)
    return pl.pallas_call(
        functools.partial(attend_kernel, members, apart),
        in_specs=[SMEM] + [ANY] * members,
        out_specs=[VMEM] * members if apart else VMEM,
        out_shape=[block] * members if apart else jax.ShapeDtypeStruct(whole, BF16),
        scratch_shapes=[pltpu.VMEM(whole, BF16)] * apart
        + [pltpu.VMEM((members * rows, 2 * HEAD_DIM), BF16)] * 3
        + [pltpu.SemaphoreType.DMA((6 * members,))],
        compiler_params=pltpu.CompilerParams(vmem_limit_bytes=40 * 2**20),
        name="attend",
    )(info, *moved)


def project_kernel(members, moved, *refs):
    last, (w, out, tangent, held, tiles, sems, tile_sems) = refs[:members], refs[members:]
    _, size, _, rows, _ = moved.shape
    rounds = size + last[0].shape[0]
    width = tiles.shape[2]
    step, steps = pl.program_id(0), pl.num_programs(0)

    def load(n):
        at = pl.ds(pl.multiple_of(n * width, width), width)
        slot = lax.rem(n, 2)
        return pltpu.make_async_copy(w.at[:, at], tiles.at[slot], tile_sems.at[slot])

    @pl.when(step == 0)
    def _():
        load(step).start()
        pairs = []
        for b in range(members):
            u = member(b, members, True)
            for r in range(rounds):
                for which in range(2):
                    source = moved.at[b, r, which] if r < size else last[b].at[r - size, which]
                    head = (b if r < size else u) * rounds + r
                    at = pl.ds(pl.multiple_of(head * HEAD_DIM, HEAD_DIM), HEAD_DIM)
                    pairs.append((source, held.at[which * rows : (which + 1) * rows, at]))
        run_copies(pairs, sems)

    @pl.when(step + 1 < steps)
    def _():
        load(step + 1).start()

    load(step).wait()
    product = jnp.dot(held[...], tiles[lax.rem(step, 2)], preferred_element_type=jnp.float32)
    out[...] = product[:rows].astype(BF16)
    tangent[...] = product[rows:].astype(BF16)


def project(moved, last, weight):
    members, size, _, rows, _ = moved.shape
    depth, width = weight.shape
    tile = 512
    given = pl.BlockSpec((rows, tile), lambda step: (0, step))
    return pl.pallas_call(
        functools.partial(project_kernel, members),
        grid=(width // tile,),
        in_specs=[ANY] * (2 + members),
        out_specs=[given, given],
        out_shape=[jax.ShapeDtypeStruct((rows, width), BF16)] * 2,
        scratch_shapes=[
            pltpu.VMEM((2 * rows, depth), BF16),
            pltpu.VMEM((2, depth, tile), BF16),
            pltpu.SemaphoreType.DMA((2 * depth // HEAD_DIM,)),
            pltpu.SemaphoreType.DMA((2,)),
        ],
        compiler_params=pltpu.CompilerParams(vmem_limit_bytes=40 * 2**20),
        name="project",
    )(moved, *last, weight)


def after(value, *done):
    return lax.optimization_barrier((value, done))[0]


def hop(value, k, f=0):
    members = lax.axis_size("ulysses")
    pairs = [(u, (u + k * CORES) % members ^ f) for u in range(members)]
    return lax.ppermute(value, "ulysses", pairs)


def gather_line(shard, ready):
    u = lax.axis_index("ulysses")
    x, core = u // CORES, u % CORES
    line = lax.axis_size("ulysses") // CORES
    back = [hop(shard, k) for k in range(line - 1, 0, -1)]
    back = after(tuple(back), ready)
    ring = jnp.stack([*back, shard] * 2)
    mine = lax.dynamic_slice_in_dim(ring, line - 1 - x, line, 0)
    theirs = hop(mine, 0, 1)
    pair = [jnp.where(core == 0, mine, theirs), jnp.where(core == 0, theirs, mine)]
    return jnp.stack(pair, axis=1).reshape(-1, shard.shape[1])


def exchange(x):
    return lax.all_to_all(x, "ulysses", split_axis=0, concat_axis=0, tiled=True)


def send(blocks):
    return {b: hop(block, b // CORES, b % CORES) if b else block for b, block in blocks.items()}


def shards(q, k, v, dq, dk, dv, out_weight, frame_counts, token_offsets, video_group):
    members = lax.axis_size("ulysses")
    rounds = q.shape[1] // HEAD_DIM // members
    tensors = (q, k, v, dq, dk, dv)
    same = tuple(range(CORES, members, CORES))
    other = tuple(range(CORES + 1, members, CORES)) + (1, 0)

    def packed(first, size, blocks):
        return dict(zip(blocks, pack(tensors, first, size, rounds, members, blocks)))

    def in_order(arrived):
        return [arrived[b] for b in range(members)]

    early = packed(0, rounds - 1, same) | packed(0, rounds - 1, other)
    near = gather_line(out_weight, early)
    weight = lax.all_gather(near, "dp", axis=0, tiled=True)
    arrived = in_order(send(early))
    mine = video_group == lax.axis_index("dp")
    info = jnp.stack(
        [
            jnp.sum(jnp.where(mine & (token_offsets == 0), frame_counts, 0)),
            jnp.sum(jnp.where(mine & (token_offsets > 0), frame_counts, 0)),
        ]
    ).astype(jnp.int32)
    late = packed(rounds - 1, 1, same + other)
    ready = [arrived[b] for b in same]
    late, ready = lax.optimization_barrier((late, ready))
    arrived = [ready[same.index(b)] if b in same else arrived[b] for b in range(members)]
    late, result = in_order(send(late)), attend(info, arrived)
    result, late = lax.optimization_barrier((result, late))
    moved = exchange(result)
    last = send(dict(enumerate(attend(info, late, True))))
    return tuple(project(moved, in_order(last), weight))


def solution(mesh):
    split = P(("dp", "ulysses"), None)
    return jax.shard_map(
        shards,
        mesh=mesh,
        in_specs=(split,) * 7 + (P(),) * 3,
        out_specs=(split, split),
        check_vma=False,
    )
```

```python
import functools
import math

import jax
import jax.numpy as jnp
from jax import lax
from jax.experimental import pallas as pl
from jax.experimental.pallas import tpu as pltpu
from jax.sharding import PartitionSpec as P

HEAD_DIM = 128
FRAME = 128
FRAMES_MOST = 8
CORES = 2
LOG2E = 1.4426950408889634
BF16 = jnp.bfloat16
ANY = pl.BlockSpec(memory_space=pl.ANY)
SMEM = pl.BlockSpec(memory_space=pltpu.SMEM)
VMEM = pl.BlockSpec(memory_space=pltpu.VMEM)


def run_copies(pairs, sems):
    copies = [pltpu.make_async_copy(a, b, sems.at[i]) for i, (a, b) in enumerate(pairs)]
    for copy in copies:
        copy.start()
    for copy in copies:
        copy.wait()


def member(block, members, back=False):
    u = lax.axis_index("ulysses")
    x, c = lax.div(u, CORES), lax.rem(u, CORES)
    line = members // CORES
    k, f = block // CORES, block % CORES
    return lax.rem(x + (line - k if back else k), line) * CORES + (1 - c if f else c)


def pack_kernel(first, rounds, members, blocks, *refs):
    tensors, outs, (held, sems, out_sems) = refs[:6], refs[6:-3], refs[-3:]
    size = outs[0].shape[0]
    loads, stores = [], []
    for j, b in enumerate(blocks):
        for i in range(size):
            head = member(b, members) * rounds + first + i
            at = pl.ds(pl.multiple_of(head * HEAD_DIM, HEAD_DIM), HEAD_DIM)
            for t in range(6):
                source, to = tensors[t].at[:, at], held.at[j, i, t]
                loads.append(pltpu.make_async_copy(source, to, sems.at[j, i, t]))
        stores.append(pltpu.make_async_copy(held.at[j], outs[j], out_sems.at[j]))
    for load in loads:
        load.start()
    for j, store in enumerate(stores):
        for load in loads[j * size * 6 : (j + 1) * size * 6]:
            load.wait()
        store.start()
    for store in stores:
        store.wait()


def pack(tensors, first, size, rounds, members, blocks):
    rows = tensors[0].shape[0]
    count = len(blocks)
    return pl.pallas_call(
        functools.partial(pack_kernel, first, rounds, members, blocks),
        in_specs=[ANY] * 6,
        out_specs=[ANY] * count,
        out_shape=[jax.ShapeDtypeStruct((size, 6, rows, HEAD_DIM), BF16)] * count,
        scratch_shapes=[
            pltpu.VMEM((count, size, 6, rows, HEAD_DIM), BF16),
            pltpu.SemaphoreType.DMA((count, size, 6)),
            pltpu.SemaphoreType.DMA((count,)),
        ],
        name="pack",
    )(*tensors)


def nt_dot(a, b):
    return lax.dot_general(a, b, (((1,), (1,)), ((), ())), preferred_element_type=jnp.float32)


def attend_kernel(members, apart, info, *refs):
    moved, outs, (qq, kk, vv, sems) = refs[:members], refs[members:-4], refs[-4:]
    if apart:
        *outs, out = outs
    else:
        (out,) = outs
    size, _, rows, _ = moved[0].shape
    per = rows // FRAME
    first_count, second_count = info[0], info[1]
    used = first_count + second_count
    factor = LOG2E / math.sqrt(HEAD_DIM)
    scale = 1.0 / math.sqrt(HEAD_DIM)

    def store(head, frame, which, value):
        at = pl.multiple_of(lax.rem(frame, per) * FRAME, FRAME)
        out[lax.div(frame, per), head, which, pl.ds(at, FRAME), :] = value

    def one_video(head, start, count):
        keys = pl.ds(pl.multiple_of(start * FRAME, FRAME), count * FRAME)

        def block(frame, frames):
            at = pl.ds(pl.multiple_of(frame * FRAME, FRAME), frames * FRAME)
            s = nt_dot(qq[at, HEAD_DIM:], kk[keys, :HEAD_DIM]) * factor
            t = nt_dot(qq[at, :], kk[keys, :]) * scale
            e = jnp.exp2(s - jnp.max(s, axis=1, keepdims=True))
            p = e * (1.0 / jnp.sum(e, axis=1, keepdims=True))
            mean = jnp.sum(p * t, axis=1, keepdims=True)
            low = p.astype(BF16)
            turned = (p * (t - mean)).astype(BF16)
            both = jnp.dot(low, vv[keys, :], preferred_element_type=jnp.float32)
            more = jnp.dot(turned, vv[keys, :HEAD_DIM], preferred_element_type=jnp.float32)
            primal = both[:, :HEAD_DIM].astype(BF16)
            tangent = (both[:, HEAD_DIM:] + more).astype(BF16)
            for i in range(frames):
                part = slice(i * FRAME, (i + 1) * FRAME)
                store(head, frame + i, 0, primal[part])
                store(head, frame + i, 1, tangent[part])

        def four_frames(i, carry):
            block(start + 4 * i, 4)
            return carry

        lax.fori_loop(0, count // 4, four_frames, 0)
        if count % 4 >= 2:
            block(start + count - count % 4, 2)
        if count % 2:
            block(start + count - 1, 1)

    def one_head(head, carry):
        pairs = []
        for b in range(members):
            at = pl.ds(pl.multiple_of(member(b, members, True) * rows, rows), rows)
            for t, (to, half) in enumerate(((qq, 1), (kk, 0), (vv, 0), (qq, 0), (kk, 1), (vv, 1))):
                part = slice(half * HEAD_DIM, (half + 1) * HEAD_DIM)
                pairs.append((moved[b].at[head, t], to.at[at, part]))
        run_copies(pairs, sems)

        def video(i, carry):
            start = jnp.where(i == 0, 0, first_count)
            count = jnp.where(i == 0, first_count, second_count)
            for frames in range(1, FRAMES_MOST + 1):
                pl.when(count == frames)(functools.partial(one_video, head, start, frames))
            return carry

        def blank(frame, carry):
            nothing = jnp.zeros((FRAME, HEAD_DIM), BF16)
            store(head, frame, 0, nothing)
            store(head, frame, 1, nothing)
            return carry

        lax.fori_loop(0, 2, video, 0)
        lax.fori_loop(used, members * per, blank, 0)
        return carry

    lax.fori_loop(0, size, one_head, 0)
    if apart:
        for b in range(members):
            outs[b][...] = out[member(b, members)]


def attend(info, moved, apart=False):
    members = len(moved)
    size, _, rows, _ = moved[0].shape
    whole = (members, size, 2, rows, HEAD_DIM)
    block = jax.ShapeDtypeStruct(whole[1:], BF16)
    return pl.pallas_call(
        functools.partial(attend_kernel, members, apart),
        in_specs=[SMEM] + [ANY] * members,
        out_specs=[VMEM] * members if apart else VMEM,
        out_shape=[block] * members if apart else jax.ShapeDtypeStruct(whole, BF16),
        scratch_shapes=[pltpu.VMEM(whole, BF16)] * apart
        + [pltpu.VMEM((members * rows, 2 * HEAD_DIM), BF16)] * 3
        + [pltpu.SemaphoreType.DMA((6 * members,))],
        compiler_params=pltpu.CompilerParams(vmem_limit_bytes=40 * 2**20),
        name="attend",
    )(info, *moved)


def project_kernel(members, moved, *refs):
    last, (w, out, tangent, held, tiles, sems, tile_sems) = refs[:members], refs[members:]
    _, size, _, rows, _ = moved.shape
    rounds = size + last[0].shape[0]
    width = tiles.shape[2]
    step, steps = pl.program_id(0), pl.num_programs(0)

    def load(n):
        at = pl.ds(pl.multiple_of(n * width, width), width)
        slot = lax.rem(n, 2)
        return pltpu.make_async_copy(w.at[:, at], tiles.at[slot], tile_sems.at[slot])

    def rows_of(which):
        copies = []
        for b in range(members):
            u = member(b, members, True)
            for r in range(rounds):
                source = moved.at[b, r, which] if r < size else last[b].at[r - size, which]
                head = (b if r < size else u) * rounds + r
                at = pl.ds(pl.multiple_of(head * HEAD_DIM, HEAD_DIM), HEAD_DIM)
                to = held.at[which * rows : (which + 1) * rows, at]
                copies.append(pltpu.make_async_copy(source, to, sems.at[which, len(copies)]))
        return copies

    @pl.when(step == 0)
    def _():
        load(step).start()
        for which in range(2):
            for copy in rows_of(which):
                copy.start()

    @pl.when(step + 1 < steps)
    def _():
        load(step + 1).start()

    def product(which):
        @pl.when(step == 0)
        def _():
            for copy in rows_of(which):
                copy.wait()

        part = held[which * rows : (which + 1) * rows, :]
        tile = tiles[lax.rem(step, 2)]
        return jnp.dot(part, tile, preferred_element_type=jnp.float32).astype(BF16)

    load(step).wait()
    out[...] = product(0)
    tangent[...] = product(1)


def project(moved, last, weight):
    members, size, _, rows, _ = moved.shape
    depth, width = weight.shape
    tile = 768
    given = pl.BlockSpec((rows, tile), lambda step: (0, step))
    return pl.pallas_call(
        functools.partial(project_kernel, members),
        grid=(width // tile,),
        in_specs=[ANY] * (2 + members),
        out_specs=[given, given],
        out_shape=[jax.ShapeDtypeStruct((rows, width), BF16)] * 2,
        scratch_shapes=[
            pltpu.VMEM((2 * rows, depth), BF16),
            pltpu.VMEM((2, depth, tile), BF16),
            pltpu.SemaphoreType.DMA((2, depth // HEAD_DIM)),
            pltpu.SemaphoreType.DMA((2,)),
        ],
        compiler_params=pltpu.CompilerParams(vmem_limit_bytes=40 * 2**20),
        name="project",
    )(moved, *last, weight)


def after(value, *done):
    return lax.optimization_barrier((value, done))[0]


def hop(value, k, f=0):
    members = lax.axis_size("ulysses")
    pairs = [(u, (u + k * CORES) % members ^ f) for u in range(members)]
    return lax.ppermute(value, "ulysses", pairs)


def gather_line(shard, ready):
    u = lax.axis_index("ulysses")
    x, core = u // CORES, u % CORES
    line = lax.axis_size("ulysses") // CORES
    back = [hop(shard, k) for k in range(line - 1, 0, -1)]
    back = after(tuple(back), ready)
    ring = jnp.stack([*back, shard] * 2)
    mine = lax.dynamic_slice_in_dim(ring, line - 1 - x, line, 0)
    theirs = hop(mine, 0, 1)
    pair = [jnp.where(core == 0, mine, theirs), jnp.where(core == 0, theirs, mine)]
    return jnp.stack(pair, axis=1).reshape(-1, shard.shape[1])


def exchange(x):
    return lax.all_to_all(x, "ulysses", split_axis=0, concat_axis=0, tiled=True)


def send(blocks):
    return {b: hop(block, b // CORES, b % CORES) if b else block for b, block in blocks.items()}


def shards(q, k, v, dq, dk, dv, out_weight, frame_counts, token_offsets, video_group):
    members = lax.axis_size("ulysses")
    rounds = q.shape[1] // HEAD_DIM // members
    tensors = (q, k, v, dq, dk, dv)
    same = tuple(range(CORES, members, CORES))
    other = tuple(range(CORES + 1, members, CORES)) + (1, 0)

    def packed(first, size, blocks):
        return dict(zip(blocks, pack(tensors, first, size, rounds, members, blocks)))

    def in_order(arrived):
        return [arrived[b] for b in range(members)]

    early = packed(0, rounds - 1, same) | packed(0, rounds - 1, other)
    near = gather_line(out_weight, early)
    weight = lax.all_gather(near, "dp", axis=0, tiled=True)
    arrived = in_order(send(early))
    mine = video_group == lax.axis_index("dp")
    info = jnp.stack(
        [
            jnp.sum(jnp.where(mine & (token_offsets == 0), frame_counts, 0)),
            jnp.sum(jnp.where(mine & (token_offsets > 0), frame_counts, 0)),
        ]
    ).astype(jnp.int32)
    late = packed(rounds - 1, 1, same + other)
    ready = [arrived[b] for b in same]
    late, ready = lax.optimization_barrier((late, ready))
    arrived = [ready[same.index(b)] if b in same else arrived[b] for b in range(members)]
    late, result = in_order(send(late)), attend(info, arrived)
    result, late = lax.optimization_barrier((result, late))
    moved = exchange(result)
    last = send(dict(enumerate(attend(info, late, True))))
    return tuple(project(moved, in_order(last), weight))


def solution(mesh):
    split = P(("dp", "ulysses"), None)
    return jax.shard_map(
        shards,
        mesh=mesh,
        in_specs=(split,) * 7 + (P(),) * 3,
        out_specs=(split, split),
        check_vma=False,
    )
```
